256 devices in a mesh: seq: 16 (over z, y_lo), tensor: 16 (over x, y_hi, core).
Axes of the slice: x: 4, y: 4 (y_hi: 2, y_lo: 2; y = y_hi * 2 + y_lo), z: 8, core: 2. Of those that a mesh axis runs over, the one named last changes fastest.
Arguments:
- tokens: bfloat16 [2048, 8192], P('tensor', 'seq'), may hold values from -6 to 6
- gate_codes: bfloat16 [8192, 28672], P('seq', 'tensor'), may hold values from -127 to 127, as said below
- up_codes: bfloat16 [8192, 28672], P('seq', 'tensor'), may hold values from -127 to 127, as said below
- down_codes: bfloat16 [28672, 8192], P('tensor', 'seq'), may hold values from -127 to 127, as said below
- gate_scale: int32 [28672], P('tensor'), may hold values from 1024 to 8191
- up_scale: int32 [28672], P('tensor'), may hold values from 1024 to 8191
- down_scale: int32 [8192], P('seq'), may hold values from 512 to 4095
- sign_bits: int32 [28672], P('tensor'), may hold values from 0 to 1
Outputs:
- ffn_output: bfloat16 [2048, 8192], P('tensor', 'seq')
The draws below stay inside these ranges and needn't reach their ends.
Inputs may be any that keep to these rules, and one draw needn't show every extreme that they name: `gate_codes`: whole numbers. `up_codes`: whole numbers. `down_codes`: whole numbers.
All inputs are finite; a program needn't handle non-finite values.
Results may differ from the reference program's by a relative error of at most 0.039.
Values may be sent and summed in bfloat16 or wider, within the bound.
A program may use at most 128 MiB of HBM per device.

```python
import math
import jax
import jax.numpy as jnp
from jax import lax

D = 8192
FF = 28672
BLOCK = 256
TOKENS = 2048
N_SEQ = 16
N_TENSOR = 16


def draw_integer_codes(key, row_count, col_count):
    values = jax.random.randint(key, (row_count, col_count), -127, 128, dtype=jnp.int32)
    return values.astype(jnp.float32).astype(jnp.bfloat16)


def draw_gate_codes(key, part):
    key = jax.random.fold_in(key, 11)
    return draw_integer_codes(key, D, FF)


def draw_up_codes(key, part):
    key = jax.random.fold_in(key, 23)
    return draw_integer_codes(key, D, FF)


def draw_down_codes(key, part):
    key = jax.random.fold_in(key, 37)
    return draw_integer_codes(key, FF, D)


def with_ends(values, key, smallest, top_value):
    shape = values.shape
    index_at = [jax.random.randint(jax.random.fold_in(key, axis), (), 0, shape[axis]) for axis in range(len(shape))]
    values = values.at[tuple(index_at)].set(smallest)
    longest = shape.index(max(shape))
    index_at[longest] = (index_at[longest] + 1) % shape[longest]
    return values.at[tuple(index_at)].set(top_value)


def block_scale(own_key, dims, pieces, smallest, top_value):
    gain = 1.0
    for dim, shards_of in pieces:
        draws = jax.random.uniform(jax.random.fold_in(jax.random.fold_in(own_key, 6), dim), (shards_of,), jnp.float32, smallest / len(pieces), top_value / len(pieces))
        gain = gain * jnp.repeat(jnp.exp(draws), dims[dim] // shards_of).reshape((-1,) + (1,) * (len(dims) - 1 - dim))
    return gain


def normal_values(own_key, shape, spread, limit, pieces=(), kind=jnp.bfloat16):
    values = jax.random.normal(own_key, shape, jnp.float32) * spread
    if len(pieces) > 0:
        values = block_scale(own_key, shape, pieces, -0.22, 0.18) * values
    return jnp.clip(values, min=-limit, max=limit).astype(kind)


def setup_inputs(seed: int = 0) -> dict:
    seeds = jax.random.split(jax.random.key(seed), 9)
    tokens = normal_values(seeds[0], (TOKENS, D), 1.0, 6.0, ((0, 16), (1, 16)))
    gate_codes = draw_gate_codes(jax.random.fold_in(seeds[8], 71), 0)
    up_codes = draw_up_codes(jax.random.fold_in(seeds[8], 71), 0)
    down_codes = draw_down_codes(jax.random.fold_in(seeds[8], 71), 0)
    gate_scale = with_ends(jax.random.randint(seeds[4], (FF,), 1024, 8192), jax.random.fold_in(seeds[4], 1), 1024, 8191).astype(jnp.int32)
    up_scale = with_ends(jax.random.randint(seeds[5], (FF,), 1024, 8192), jax.random.fold_in(seeds[5], 1), 1024, 8191).astype(jnp.int32)
    down_scale = with_ends(jax.random.randint(seeds[6], (D,), 512, 4096), jax.random.fold_in(seeds[6], 1), 512, 4095).astype(jnp.int32)
    sign_bits = with_ends(jax.random.randint(seeds[7], (FF,), 0, 2), jax.random.fold_in(seeds[7], 1), 0, 1).astype(jnp.int32)
    return dict(tokens=tokens, gate_codes=gate_codes, up_codes=up_codes, down_codes=down_codes, gate_scale=gate_scale, up_scale=up_scale, down_scale=down_scale, sign_bits=sign_bits)


CODE_SCALE = 2.0 ** (-24)

def walsh_table(extent):
    row_ids = jnp.arange(extent, dtype=jnp.int32)[:, None]
    col_ids = jnp.arange(extent, dtype=jnp.int32)[None, :]
    common = jnp.bitwise_and(row_ids, col_ids)
    parity = jnp.zeros((extent, extent), jnp.int32)
    for bit_pos in range(max(extent.bit_length() - 1, 1)):
        parity = jnp.bitwise_xor(parity, jnp.bitwise_and(jnp.right_shift(common, bit_pos), 1))
    return (1 - 2 * parity).astype(jnp.float32)

def rounded(value):
    return lax.optimization_barrier(value.astype(jnp.bfloat16)).astype(jnp.float32)

def reference(tokens, gate_codes, up_codes, down_codes, gate_scale, up_scale, down_scale, sign_bits):
    gate_factor = gate_scale.astype(jnp.float32) * CODE_SCALE
    up_factor = up_scale.astype(jnp.float32) * CODE_SCALE
    down_factor = down_scale.astype(jnp.float32) * CODE_SCALE
    group_depth = D // N_SEQ
    gate_sum = jnp.zeros((TOKENS, FF), jnp.float32)
    up_sum = jnp.zeros((TOKENS, FF), jnp.float32)
    for group_index in range(N_SEQ):
        first_col = group_index * group_depth
        window = tokens[:, first_col:first_col + group_depth]
        gate_sum = gate_sum + rounded(jnp.dot(window, gate_codes[first_col:first_col + group_depth], preferred_element_type=jnp.float32) * gate_factor)
        up_sum = up_sum + rounded(jnp.dot(window, up_codes[first_col:first_col + group_depth], preferred_element_type=jnp.float32) * up_factor)
    hidden = jax.nn.silu(gate_sum) * up_sum * (2 * sign_bits - 1).astype(jnp.float32)
    blocks = hidden.reshape(TOKENS, FF // BLOCK, BLOCK)
    turned = jnp.einsum('rbk,kj->rbj', blocks, walsh_table(BLOCK), precision=lax.Precision.HIGHEST) * (1.0 / math.sqrt(BLOCK))
    group_width = FF // N_TENSOR
    local_rot = rounded(turned.reshape(TOKENS, N_TENSOR, group_width))
    combined = jnp.einsum('pq,tqc->tpc', walsh_table(N_TENSOR), local_rot, precision=lax.Precision.HIGHEST) * (1.0 / math.sqrt(N_TENSOR))
    rotated = combined.astype(jnp.bfloat16).reshape(TOKENS, FF)
    down_sum = jnp.zeros((TOKENS, D), jnp.float32)
    for group_index in range(N_TENSOR):
        first_row = group_index * group_width
        down_sum = down_sum + rounded(jnp.dot(rotated[:, first_row:first_row + group_width], down_codes[first_row:first_row + group_width], preferred_element_type=jnp.float32) * down_factor)
    return down_sum.astype(jnp.bfloat16)
```

```python
import functools
import math

import jax
import jax.numpy as jnp
import numpy as np
from jax import lax
from jax.experimental import pallas as pl
from jax.experimental.pallas import tpu as pltpu
from jax.sharding import PartitionSpec as P

BLOCK = 256
TILE = 128
ROWS = 16
YL = 2
CORES = 2
CODE_SCALE = 2.0 ** (-24)
MESH = pl.DeviceIdType.MESH
F32 = jnp.float32
BF16 = jnp.bfloat16


def walsh(extent):
    ids = np.arange(extent)
    common = ids[:, None] & ids[None, :]
    parity = np.zeros_like(common)
    while common.any():
        parity ^= common & 1
        common = common >> 1
    return (1 - 2 * parity).astype(np.float32)


def kernel(
    cfg,
    tok_hbm, gate_hbm, up_hbm, down_hbm, fac_hbm, dfac_ref, walsh_ref,
    out_ref,
    tok, wv, dv, fac, part, ring, lr, ar, br, agr, dp, dr,
    tok_s, tok_r, wa, wb, w_s, wf_s, d_a, d_b, d_s, df_s, fac_r, fac_s,
    ring_s, ring_r, a_s, a_r, b_s, b_r, g_s, g_r, o_s, o_r,
):
    Z, K, NCH = cfg
    NP = K * YL
    half = Z // 2
    seq = lax.axis_index("seq")
    ten = lax.axis_index("tensor")
    z = seq // YL
    a = lax.rem(seq, YL)
    k = ten // CORES
    c = lax.rem(ten, CORES)
    me = k * YL + a
    diag = a == c

    def plane(p):
        return (z * YL + lax.rem(p, YL), (p // YL) * CORES + c)

    def ring_dev(d):
        step = 1 if d == 0 else Z - 1
        return (lax.rem(z + step, Z) * YL + a, ten)

    other_core = (seq, k * CORES + (1 - c))
    other_y = (z * YL + (1 - a), ten)

    def remote(src, dst, ss, rs, dev):
        return pltpu.make_async_remote_copy(
            src_ref=src, dst_ref=dst, send_sem=ss, recv_sem=rs,
            device_id=dev, device_id_type=MESH)

    barrier = pltpu.get_barrier_semaphore()

    def greet(i, _):
        pl.semaphore_signal(barrier, inc=1, device_id=plane(lax.rem(me + i, NP)), device_id_type=MESH)
        return 0

    lax.fori_loop(1, NP, greet, 0)
    pl.semaphore_signal(barrier, inc=1, device_id=other_core, device_id_type=MESH)
    for d in range(2):
        pl.semaphore_signal(barrier, inc=1, device_id=ring_dev(d), device_id_type=MESH)
    pl.semaphore_wait(barrier, NP - 1 + 3)

    def tok_copy(i):
        return remote(tok_hbm, tok.at[a, :, k], tok_s.at[i], tok_r.at[i], plane(lax.rem(me + i, NP)))

    def tok_start(i, _):
        tok_copy(i).start()
        return 0

    lax.fori_loop(1, NP, tok_start, 0)
    tok_own = pltpu.make_async_copy(tok_hbm, tok.at[a, :, k], tok_s.at[0])
    tok_own.start()

    def chunk_of(ref, ch):
        return ref.at[:, pl.ds(pl.multiple_of(ch * BLOCK, BLOCK), BLOCK)]

    def w_start(ch):
        for g, ref in enumerate((gate_hbm, up_hbm)):
            src = chunk_of(ref, ch)
            dst = wv.at[ch, a, g]

            @pl.when(diag)
            def _():
                pltpu.make_async_copy(src, dst, wa.at[ch]).start()
                remote(src, dst, w_s.at[ch], wa.at[ch], other_core).start()

            @pl.when(jnp.logical_not(diag))
            def _():
                remote(src, dst, w_s.at[ch], wb.at[ch], other_y).start()

    def w_wait(ch):
        pltpu.make_async_copy(wv.at[ch, a], wv.at[ch, a], wa.at[ch]).wait()
        pltpu.make_async_copy(wv.at[ch, 1 - a], wv.at[ch, 1 - a], wb.at[ch]).wait()

    def w_forward(ch):
        return remote(wv.at[ch, 1 - a], wv.at[ch, 1 - a], wf_s.at[ch], wb.at[ch], other_core)

    def d_start():
        for h in range(2):
            src = down_hbm.at[:, h]
            dst = dv.at[a, h]

            @pl.when(diag)
            def _():
                pltpu.make_async_copy(src, dst, d_a).start()
                remote(src, dst, d_s, d_a, other_core).start()

            @pl.when(jnp.logical_not(diag))
            def _():
                remote(src, dst, d_s, d_b, other_y).start()

    def d_forward():
        return remote(dv.at[1 - a], dv.at[1 - a], df_s, d_b, other_core)

    ahead = min(3, NCH)
    for ch in range(ahead):
        w_start(ch)

    @pl.when(diag)
    def _():
        pltpu.make_async_copy(fac_hbm, fac, fac_r).start()
        remote(fac_hbm, fac, fac_s, fac_r, other_core).start()

    pltpu.make_async_copy(fac, fac, fac_r).wait()

    def tok_wait(i, _):
        tok_copy(i).wait_recv()
        return 0

    lax.fori_loop(1, NP, tok_wait, 0)
    tok_own.wait()

    def ring_copy(d, ch, n):
        step = half - n if d == 0 else Z - half + n
        j = lax.rem(z + step, Z)
        if n == 0:
            return remote(part.at[ch, j, d], ring.at[d, ch, n, d], ring_s.at[d, ch, n], ring_r.at[d, ch, n], ring_dev(d))
        return remote(part.at[ch, j], ring.at[d, ch, n], ring_s.at[d, ch, n], ring_r.at[d, ch, n], ring_dev(d))

    def first(ch):
        w_wait(ch)

        @pl.when(diag)
        def _():
            w_forward(ch).start()

        def rows(m, _):
            for g in range(2):
                acc = jnp.zeros((2 * K * ROWS, BLOCK), F32)
                for f in range(2):
                    x = tok[f, pl.ds(2 * m, 2)].reshape(2 * K * ROWS, -1)
                    acc += jnp.dot(x, wv[ch, f, g], preferred_element_type=F32)
                part[ch, pl.ds(2 * m, 2), g] = acc.astype(BF16).reshape(2, K * ROWS, BLOCK)
            return 0

        lax.fori_loop(0, Z // 2, rows, 0)
        for d in range(2):
            ring_copy(d, ch, 0).start()

        @pl.when(ch + ahead < NCH)
        def _():
            w_start(ch + ahead)

        @pl.when(ch == NCH - 1)
        def _():
            d_start()

    def middle(ch, n):
        for d in range(2):
            ring_copy(d, ch, n - 1).wait_recv()
            step = half - n if d == 0 else Z - half + n
            j = lax.rem(z + step, Z)
            for g in ((d,) if n == 1 else (0, 1)):
                part[ch, j, g] = (part[ch, j, g].astype(F32) + ring[d, ch, n - 1, g].astype(F32)).astype(BF16)
            ring_copy(d, ch, n).start()

    def last(ch):
        n = half - 1
        for d in range(2):
            ring_copy(d, ch, n).wait_recv()
        sums = [
            part[ch, z, g].astype(F32) + ring[0, ch, n, g].astype(F32) + ring[1, ch, n, g].astype(F32)
            for g in range(2)
        ]
        table = fac[ch]
        gate = sums[0] * table[0:1]
        up = sums[1] * table[1:2]
        hidden = gate / (1.0 + jnp.exp(-gate)) * up * table[2:3]
        hi = hidden.astype(BF16)
        lo = (hidden - hi.astype(F32)).astype(BF16)
        w = walsh_ref[...]
        turned = jnp.dot(hi, w, preferred_element_type=F32) + jnp.dot(lo, w, preferred_element_type=F32)
        turned = (turned * (1.0 / math.sqrt(BLOCK))).astype(BF16)
        for h in range(2):
            lr[ch, h] = turned[:, h * TILE:(h + 1) * TILE].reshape(K, ROWS, TILE)

    def slot(t, _):
        for n in range(half, -1, -1):
            ch = t - n

            @pl.when(jnp.logical_and(ch >= 0, ch < NCH))
            def _():
                if n == 0:
                    first(ch)
                elif n == half:
                    last(ch)
                else:
                    middle(ch, n)

        return 0

    lax.fori_loop(0, NCH + half, slot, 0)

    my_r, my_h = me // 2, lax.rem(me, 2)

    def a_copy(i):
        p = lax.rem(me + i, NP)
        return remote(lr.at[:, lax.rem(p, 2), p // 2], ar.at[me], a_s.at[i], a_r.at[i], plane(p))

    def a_start(i, _):
        a_copy(i).start()
        return 0

    lax.fori_loop(1, NP, a_start, 0)
    ar[me] = lr[:, my_h, my_r]

    def a_wait(i, _):
        a_copy(i).wait_recv()
        return 0

    lax.fori_loop(1, NP, a_wait, 0)

    def mix(ch, _):
        vals = [ar[q, ch].astype(F32) for q in range(NP)]
        bit = 1
        while bit < NP:
            nxt = list(vals)
            for q in range(NP):
                if not q & bit:
                    nxt[q] = vals[q] + vals[q | bit]
                    nxt[q | bit] = vals[q] - vals[q | bit]
            vals = nxt
            bit *= 2
        for q in range(NP):
            br[q, :, pl.ds(pl.multiple_of(ch * TILE, TILE), TILE)] = (vals[q] * (1.0 / math.sqrt(NP))).astype(BF16)
        return 0

    lax.fori_loop(0, NCH, mix, 0)

    def b_copy(i):
        p = lax.rem(me + i, NP)
        return remote(br.at[p], agr.at[z, my_h, my_r], b_s.at[i], b_r.at[i], plane(p))

    def b_start(i, _):
        b_copy(i).start()
        return 0

    lax.fori_loop(1, NP, b_start, 0)
    agr[z, my_h, my_r] = br[me]

    pltpu.make_async_copy(dv.at[a], dv.at[a], d_a).wait()
    pltpu.make_async_copy(dv.at[1 - a], dv.at[1 - a], d_b).wait()

    @pl.when(diag)
    def _():
        d_forward().start()

    def b_wait(i, _):
        b_copy(i).wait_recv()
        return 0

    lax.fori_loop(1, NP, b_wait, 0)

    def g_copy(d, n, h):
        j = lax.rem(z + (Z - n if d == 0 else n), Z)
        return remote(agr.at[j, h], agr.at[j, h], g_s.at[d, n, h], g_r.at[d, n, h], ring_dev(d))

    def g_wait(d, n, h):
        j = lax.rem(z + (2 * Z - 1 - n if d == 0 else 1 + n), Z)
        pltpu.make_async_copy(agr.at[j, h], agr.at[j, h], g_r.at[d, n, h]).wait()

    def o_copy(j, i):
        p = lax.rem(me + i, NP)
        return remote(dp.at[j, lax.rem(p, 2), p // 2], dr.at[me, j], o_s.at[i], o_r.at[i], plane(p))

    def down(j):
        for f in range(2):
            for q in range(dp.shape[-1] // BLOCK):
                cols = slice(q * BLOCK, (q + 1) * BLOCK)
                acc = jnp.zeros((K * ROWS, BLOCK), F32)
                for h in range(2):
                    x = agr[j, h].reshape(K * ROWS, NCH * TILE)
                    acc += jnp.dot(x, dv[f, h, :, :, cols].reshape(NCH * TILE, BLOCK), preferred_element_type=F32)
                dp[j, f, :, :, cols] = acc.astype(BF16).reshape(K, ROWS, BLOCK)

        def o_start(i, _):
            o_copy(j, i).start()
            return 0

        lax.fori_loop(1, NP, o_start, 0)
        dr[me, j] = dp[j, a, k]

    for h in range(2):
        for d in range(2):
            if half > 1 or h == d:
                g_copy(d, 0, h).start()
    down(z)

    def around(n, _):
        for h in range(2):
            for d in range(2):
                g_wait(d, n, h)
                if h == d:
                    g_copy(d, n + 1, h).start()
                else:
                    @pl.when(n + 1 < half - 1)
                    def _():
                        g_copy(d, n + 1, h).start()

        down(lax.rem(z + Z - 1 - n, Z))
        down(lax.rem(z + 1 + n, Z))
        return 0

    lax.fori_loop(0, half - 1, around, 0)
    for d in range(2):
        g_wait(d, half - 1, d)
    down(lax.rem(z + half, Z))

    def o_wait(i, _):
        src = lax.rem(me + NP - i, NP)
        pltpu.make_async_copy(dr.at[src], dr.at[src], o_r.at[i]).wait()
        return 0

    lax.fori_loop(1, NP, o_wait, 0)

    def total(j, _):
        acc = dr[0, j].astype(F32)
        for q in range(1, NP):
            acc += dr[q, j].astype(F32)
        out_ref[pl.ds(pl.multiple_of(j * ROWS, ROWS), ROWS), :] = (acc * dfac_ref[...]).astype(BF16)
        return 0

    lax.fori_loop(0, Z, total, 0)

    def sent(i, _):
        tok_copy(i).wait_send()
        a_copy(i).wait_send()
        b_copy(i).wait_send()
        pltpu.make_async_copy(dr.at[0], dr.at[0], o_s.at[i]).wait()
        return 0

    lax.fori_loop(1, NP, sent, 0)

    def w_sent(ch, _):
        pltpu.make_async_copy(wv.at[ch, a], wv.at[ch, a], w_s.at[ch]).wait()

        @pl.when(diag)
        def _():
            w_forward(ch).wait_send()

        for d in range(2):
            for n in range(half):
                ring_copy(d, ch, n).wait_send()
        return 0

    lax.fori_loop(0, NCH, w_sent, 0)
    pltpu.make_async_copy(dv.at[a], dv.at[a], d_s).wait()

    @pl.when(diag)
    def _():
        d_forward().wait_send()
        remote(fac_hbm, fac, fac_s, fac_r, other_core).wait_send()

    for d in range(2):
        for n in range(half):
            for h in range(2):
                if n < half - 1 or h == d:
                    g_copy(d, n, h).wait_send()


def on_device(Z, K, tokens, gate_codes, up_codes, down_codes, gate_scale, up_scale, down_scale, sign_bits):
    feats = tokens.shape[1]
    width = gate_codes.shape[1]
    NCH = width // BLOCK
    NP = K * YL
    half = Z // 2
    table = jnp.stack(
        [
            gate_scale.astype(F32) * CODE_SCALE,
            up_scale.astype(F32) * CODE_SCALE,
            (2 * sign_bits - 1).astype(F32),
        ]
        + [jnp.zeros((width,), F32)] * 5
    )
    table = table.reshape(8, NCH, BLOCK).transpose(1, 0, 2)
    dfac = (down_scale.astype(F32) * CODE_SCALE)[None]
    dma = pltpu.SemaphoreType.DMA
    any_spec = pl.BlockSpec(memory_space=pl.ANY)
    vmem_spec = pl.BlockSpec(memory_space=pltpu.VMEM)
    return pl.pallas_call(
        functools.partial(kernel, (Z, K, NCH)),
        out_shape=jax.ShapeDtypeStruct(tokens.shape, BF16),
        in_specs=[any_spec] * 5 + [vmem_spec] * 2,
        out_specs=vmem_spec,
        scratch_shapes=[
            pltpu.VMEM((2, Z, K, ROWS, feats), BF16),
            pltpu.VMEM((NCH, 2, 2, feats, BLOCK), BF16),
            pltpu.VMEM((2, 2, NCH, TILE, feats), BF16),
            pltpu.VMEM((NCH, 8, BLOCK), F32),
            pltpu.VMEM((NCH, Z, 2, K * ROWS, BLOCK), BF16),
            pltpu.VMEM((2, NCH, half, 2, K * ROWS, BLOCK), BF16),
            pltpu.VMEM((NCH, 2, K, ROWS, TILE), BF16),
            pltpu.VMEM((NP, NCH, ROWS, TILE), BF16),
            pltpu.VMEM((NP, ROWS, NCH * TILE), BF16),
            pltpu.VMEM((Z, 2, K, ROWS, NCH * TILE), BF16),
            pltpu.VMEM((Z, 2, K, ROWS, feats), BF16),
            pltpu.VMEM((NP, Z, ROWS, feats), BF16),
            dma((NP,)), dma((NP,)),
            dma((NCH,)), dma((NCH,)), dma((NCH,)), dma((NCH,)),
            dma, dma, dma, dma,
            dma, dma,
            dma((2, NCH, half)), dma((2, NCH, half)),
            dma((NP,)), dma((NP,)), dma((NP,)), dma((NP,)),
            dma((2, half, 2)), dma((2, half, 2)),
            dma((NP,)), dma((NP,)),
        ],
        compiler_params=pltpu.CompilerParams(
            collective_id=0, has_side_effects=True, vmem_limit_bytes=56 * 1024 * 1024),
    )(
        tokens.reshape(Z, ROWS, feats),
        gate_codes,
        up_codes,
        down_codes.reshape(NCH, 2, TILE, down_codes.shape[1]),
        table,
        dfac,
        jnp.asarray(walsh(BLOCK), BF16),
    )


def solution(mesh):
    Z = mesh.shape["seq"] // YL
    K = mesh.shape["tensor"] // CORES
    placed = (
        P("tensor", "seq"),
        P("seq", "tensor"),
        P("seq", "tensor"),
        P("tensor", "seq"),
        P("tensor"),
        P("tensor"),
        P("seq"),
        P("tensor"),
    )
    return jax.shard_map(
        functools.partial(on_device, Z, K), mesh=mesh, in_specs=placed, out_specs=P("tensor", "seq"), check_vma=False
    )
```

```python
import functools
import math

import jax
import jax.numpy as jnp
import numpy as np
from jax import lax
from jax.experimental import pallas as pl
from jax.experimental.pallas import tpu as pltpu
from jax.sharding import PartitionSpec as P

BLOCK = 256
TILE = 128
ROWS = 16
YL = 2
YH = 2
CORES = 2
CODE_SCALE = 2.0 ** (-24)
MESH = pl.DeviceIdType.MESH
F32 = jnp.float32
BF16 = jnp.bfloat16


def walsh(extent):
    ids = np.arange(extent)
    common = ids[:, None] & ids[None, :]
    parity = np.zeros_like(common)
    while common.any():
        parity ^= common & 1
        common = common >> 1
    return (1 - 2 * parity).astype(np.float32)


def kernel(
    cfg,
    tok_hbm, gate_hbm, up_hbm, down_hbm, gs_hbm, us_hbm, sb_hbm, ds_ref, walsh_ref,
    out_ref,
    tok, wv, dv, fac, part, ring, lr, ar, br, agr, dp, dr,
    tok_s, tok_r, tok_o, wa, wb, w_s, wf_s, d_a, d_b, d_s, df_s, fac_r, fac_s,
    ring_s, ring_r, a_s, a_r, b_s, b_r, g_s, g_r, o_s, o_r,
):
    Z, K, NCH = cfg
    NP = K * YL
    half = Z // 2
    seq = lax.axis_index("seq")
    ten = lax.axis_index("tensor")
    z = seq // YL
    a = lax.rem(seq, YL)
    k = ten // CORES
    c = lax.rem(ten, CORES)
    me = k * YL + a
    diag = a == c

    def plane(p):
        return (z * YL + lax.rem(p, YL), (p // YL) * CORES + c)

    def ring_dev(d):
        step = 1 if d == 0 else Z - 1
        return (lax.rem(z + step, Z) * YL + a, ten)

    other_core = (seq, k * CORES + (1 - c))
    other_y = (z * YL + (1 - a), ten)

    def remote(src, dst, ss, rs, dev):
        return pltpu.make_async_remote_copy(
            src_ref=src, dst_ref=dst, send_sem=ss, recv_sem=rs,
            device_id=dev, device_id_type=MESH)

    NY = YH * YL
    NX = NP // NY
    x, y = k // YH, lax.rem(k, YH) * YL + a

    def chip(cx, cy):
        return (z * YL + lax.rem(cy, YL), (cx * YH + cy // YL) * CORES + c)

    def moved(axis, by):
        if axis == 0:
            return lax.rem(x + by, NX), y
        return x, lax.rem(y + by, NY)

    barrier = pltpu.get_barrier_semaphore()
    near = [chip(*moved(0, 1)), chip(*moved(0, NX - 1)), chip(*moved(1, 1)), chip(*moved(1, NY - 1)),
            other_core, ring_dev(0), ring_dev(1)]
    for dev in near:
        pl.semaphore_signal(barrier, inc=1, device_id=dev, device_id_type=MESH)
    pl.semaphore_wait(barrier, len(near))

    feats = tok.shape[-1]
    wide = feats // 2
    tok_own = pltpu.make_async_copy(tok_hbm, tok.at[a, :, k], tok_o)

    def spot(f, cx, cy, rows=slice(None)):
        return tok.at[lax.rem(cy, YL), rows, cx * YH + cy // YL, :, f * wide:(f + 1) * wide]

    def tok_copy(f, stage, i, d, hop):
        axis = f if stage == 0 else 1 - f
        size = NX if axis == 0 else NY
        by = 1 if d == 0 else size - 1
        dev = chip(*moved(axis, by))
        back = size - 1 if d == 0 else 1
        cx, cy = moved(axis, back) if hop else (x, y)
        if stage == 1:
            if f == 0:
                cx = lax.rem(x + i, NX)
            else:
                cy = lax.rem(y + i, NY)
        rows = slice(None) if not hop else (slice(0, Z // 2) if d == 0 else slice(Z // 2, Z))
        sem = (f, 1 + i if stage == 1 else 0, d, hop)
        dst = spot(f, cx, cy, rows)
        src = tok_hbm.at[:, :, f * wide:(f + 1) * wide] if stage == 0 and not hop else dst
        if stage == 1 and not hop and i == 0:
            src = tok_hbm.at[:, :, f * wide:(f + 1) * wide]
        return remote(src, dst, tok_s.at[sem], tok_r.at[sem], dev)

    def tok_arrived(f, stage, i, d, hop):
        axis = f if stage == 0 else 1 - f
        size = NX if axis == 0 else NY
        n = 2 if hop else 1
        by = size - n if d == 0 else n
        cx, cy = moved(axis, by)
        if stage == 1:
            if f == 0:
                cx = lax.rem(x + i, NX)
            else:
                cy = lax.rem(y + i, NY)
        rows = slice(None) if not hop else (slice(0, Z // 2) if d == 0 else slice(Z // 2, Z))
        sem = (f, 1 + i if stage == 1 else 0, d, hop)
        ref = spot(f, cx, cy, rows)
        pltpu.make_async_copy(ref, ref, tok_r.at[sem]).wait()

    def tok_begin():
        for f in range(2):
            for d in range(2):
                tok_copy(f, 0, 0, d, 0).start()
        tok_own.start()
        for f in range(2):
            for d in range(2):
                tok_copy(f, 1, 0, d, 0).start()

    def tok_relay():
        for d in range(2):
            for f in range(2):
                tok_arrived(f, 0, 0, d, 0)
                tok_copy(f, 0, 0, d, 1).start()
                i = 3 if d == 0 else 1
                for e in range(2):
                    tok_copy(f, 1, i, e, 0).start()
        for f in range(2):
            for d in range(2):
                tok_arrived(f, 0, 0, d, 1)
            for e in range(2):
                tok_copy(f, 1, 2, e, 0).start()
        for i in (0, 3, 1, 2):
            for f in range(2):
                for d in range(2):
                    tok_arrived(f, 1, i, d, 0)
                    tok_copy(f, 1, i, d, 1).start()
        for i in (0, 3, 1, 2):
            for f in range(2):
                for d in range(2):
                    tok_arrived(f, 1, i, d, 1)
        tok_own.wait()

    def tok_sent():
        for f in range(2):
            for d in range(2):
                for hop in range(2):
                    tok_copy(f, 0, 0, d, hop).wait_send()
                    for i in range(4):
                        tok_copy(f, 1, i, d, hop).wait_send()

    tok_begin()

    def chunk_of(ref, ch):
        return ref.at[:, pl.ds(pl.multiple_of(ch * BLOCK, BLOCK), BLOCK)]

    def w_start(ch):
        for g, ref in enumerate((gate_hbm, up_hbm)):
            src = chunk_of(ref, ch)
            dst = wv.at[ch, a, g]

            @pl.when(diag)
            def _():
                pltpu.make_async_copy(src, dst, wa.at[ch]).start()
                remote(src, dst, w_s.at[ch], wa.at[ch], other_core).start()

            @pl.when(jnp.logical_not(diag))
            def _():
                remote(src, dst, w_s.at[ch], wb.at[ch], other_y).start()

    def w_wait(ch):
        pltpu.make_async_copy(wv.at[ch, a], wv.at[ch, a], wa.at[ch]).wait()
        pltpu.make_async_copy(wv.at[ch, 1 - a], wv.at[ch, 1 - a], wb.at[ch]).wait()

    def w_forward(ch):
        return remote(wv.at[ch, 1 - a], wv.at[ch, 1 - a], wf_s.at[ch], wb.at[ch], other_core)

    def d_start():
        for h in range(2):
            src = down_hbm.at[:, h]
            dst = dv.at[a, h]

            @pl.when(diag)
            def _():
                pltpu.make_async_copy(src, dst, d_a).start()
                remote(src, dst, d_s, d_a, other_core).start()

            @pl.when(jnp.logical_not(diag))
            def _():
                remote(src, dst, d_s, d_b, other_y).start()

    def d_forward():
        return remote(dv.at[1 - a], dv.at[1 - a], df_s, d_b, other_core)

    ahead = min(3, NCH)
    for ch in range(ahead):
        w_start(ch)

    @pl.when(diag)
    def _():
        for i, ref in enumerate((gs_hbm, us_hbm, sb_hbm)):
            pltpu.make_async_copy(ref, fac.at[i], fac_r.at[i]).start()
            remote(ref, fac.at[i], fac_s.at[i], fac_r.at[i], other_core).start()

    tok_relay()
    for i in range(3):
        pltpu.make_async_copy(fac.at[i], fac.at[i], fac_r.at[i]).wait()

    def ring_copy(d, ch, n):
        step = half - n if d == 0 else Z - half + n
        j = lax.rem(z + step, Z)
        if n == 0:
            return remote(part.at[ch, j, d], ring.at[d, ch, n, d], ring_s.at[d, ch, n], ring_r.at[d, ch, n], ring_dev(d))
        return remote(part.at[ch, j], ring.at[d, ch, n], ring_s.at[d, ch, n], ring_r.at[d, ch, n], ring_dev(d))

    def first(ch):
        w_wait(ch)

        @pl.when(diag)
        def _():
            w_forward(ch).start()

        def rows(m, _):
            for g in range(2):
                acc = jnp.zeros((2 * K * ROWS, BLOCK), F32)
                for f in range(2):
                    x = tok[f, pl.ds(2 * m, 2)].reshape(2 * K * ROWS, -1)
                    acc += jnp.dot(x, wv[ch, f, g], preferred_element_type=F32)
                part[ch, pl.ds(2 * m, 2), g] = acc.astype(BF16).reshape(2, K * ROWS, BLOCK)
            return 0

        lax.fori_loop(0, Z // 2, rows, 0)
        for d in range(2):
            ring_copy(d, ch, 0).start()

        @pl.when(ch + ahead < NCH)
        def _():
            w_start(ch + ahead)

        @pl.when(ch == NCH - 1)
        def _():
            d_start()

    def middle(ch, n):
        for d in range(2):
            ring_copy(d, ch, n - 1).wait_recv()
            step = half - n if d == 0 else Z - half + n
            j = lax.rem(z + step, Z)
            for g in ((d,) if n == 1 else (0, 1)):
                part[ch, j, g] = (part[ch, j, g].astype(F32) + ring[d, ch, n - 1, g].astype(F32)).astype(BF16)
            ring_copy(d, ch, n).start()

    def last(ch):
        n = half - 1
        for d in range(2):
            ring_copy(d, ch, n).wait_recv()
        sums = [
            part[ch, z, g].astype(F32) + ring[0, ch, n, g].astype(F32) + ring[1, ch, n, g].astype(F32)
            for g in range(2)
        ]
        gate_f, up_f, sign = [
            jnp.concatenate([fac[i, pl.ds(2 * ch + h, 1), :] for h in range(2)], axis=1) for i in range(3)
        ]
        gate = sums[0] * (gate_f.astype(F32) * CODE_SCALE)
        up = sums[1] * (up_f.astype(F32) * CODE_SCALE)
        hidden = gate / (1.0 + jnp.exp(-gate)) * up * (2 * sign - 1).astype(F32)
        hi = hidden.astype(BF16)
        lo = (hidden - hi.astype(F32)).astype(BF16)
        w = walsh_ref[...]
        turned = jnp.dot(hi, w, preferred_element_type=F32) + jnp.dot(lo, w, preferred_element_type=F32)
        turned = (turned * (1.0 / math.sqrt(BLOCK))).astype(BF16)
        for h in range(2):
            lr[ch, h] = turned[:, h * TILE:(h + 1) * TILE].reshape(K, ROWS, TILE)

    def slot(t, _):
        for n in range(half, -1, -1):
            ch = t - n

            @pl.when(jnp.logical_and(ch >= 0, ch < NCH))
            def _():
                if n == 0:
                    first(ch)
                elif n == half:
                    last(ch)
                else:
                    middle(ch, n)

        return 0

    lax.fori_loop(0, NCH + half, slot, 0)

    my_r, my_h = me // 2, lax.rem(me, 2)

    def a_copy(i):
        p = lax.rem(me + i, NP)
        return remote(lr.at[:, lax.rem(p, 2), p // 2], ar.at[me], a_s.at[i], a_r.at[i], plane(p))

    def a_start(i, _):
        a_copy(i).start()
        return 0

    lax.fori_loop(1, NP, a_start, 0)
    ar[me] = lr[:, my_h, my_r]

    def a_wait(i, _):
        a_copy(i).wait_recv()
        return 0

    lax.fori_loop(1, NP, a_wait, 0)

    def mix(ch, _):
        vals = [ar[q, ch].astype(F32) for q in range(NP)]
        bit = 1
        while bit < NP:
            nxt = list(vals)
            for q in range(NP):
                if not q & bit:
                    nxt[q] = vals[q] + vals[q | bit]
                    nxt[q | bit] = vals[q] - vals[q | bit]
            vals = nxt
            bit *= 2
        for q in range(NP):
            br[q, :, pl.ds(pl.multiple_of(ch * TILE, TILE), TILE)] = (vals[q] * (1.0 / math.sqrt(NP))).astype(BF16)
        return 0

    lax.fori_loop(0, NCH, mix, 0)

    def b_copy(i):
        p = lax.rem(me + i, NP)
        return remote(br.at[p], agr.at[z, my_h, my_r], b_s.at[i], b_r.at[i], plane(p))

    def b_start(i, _):
        b_copy(i).start()
        return 0

    lax.fori_loop(1, NP, b_start, 0)
    agr[z, my_h, my_r] = br[me]

    pltpu.make_async_copy(dv.at[a], dv.at[a], d_a).wait()
    pltpu.make_async_copy(dv.at[1 - a], dv.at[1 - a], d_b).wait()

    @pl.when(diag)
    def _():
        d_forward().start()

    def b_wait(i, _):
        b_copy(i).wait_recv()
        return 0

    lax.fori_loop(1, NP, b_wait, 0)

    def g_copy(d, n, h):
        j = lax.rem(z + (Z - n if d == 0 else n), Z)
        return remote(agr.at[j, h], agr.at[j, h], g_s.at[d, n, h], g_r.at[d, n, h], ring_dev(d))

    def g_wait(d, n, h):
        j = lax.rem(z + (2 * Z - 1 - n if d == 0 else 1 + n), Z)
        pltpu.make_async_copy(agr.at[j, h], agr.at[j, h], g_r.at[d, n, h]).wait()

    def o_copy(j, i):
        p = lax.rem(me + i, NP)
        return remote(dp.at[j, lax.rem(p, 2), p // 2], dr.at[me, j], o_s.at[i], o_r.at[i], plane(p))

    def down(j):
        for f in range(2):
            for q in range(dp.shape[-1] // BLOCK):
                cols = slice(q * BLOCK, (q + 1) * BLOCK)
                acc = jnp.zeros((K * ROWS, BLOCK), F32)
                for h in range(2):
                    x = agr[j, h].reshape(K * ROWS, NCH * TILE)
                    acc += jnp.dot(x, dv[f, h, :, :, cols].reshape(NCH * TILE, BLOCK), preferred_element_type=F32)
                dp[j, f, :, :, cols] = acc.astype(BF16).reshape(K, ROWS, BLOCK)

        def o_start(i, _):
            o_copy(j, i).start()
            return 0

        lax.fori_loop(1, NP, o_start, 0)
        dr[me, j] = dp[j, a, k]

    for h in range(2):
        for d in range(2):
            if half > 1 or h == d:
                g_copy(d, 0, h).start()
    down(z)

    def around(n, _):
        for h in range(2):
            for d in range(2):
                g_wait(d, n, h)
                if h == d:
                    g_copy(d, n + 1, h).start()
                else:
                    @pl.when(n + 1 < half - 1)
                    def _():
                        g_copy(d, n + 1, h).start()

        down(lax.rem(z + Z - 1 - n, Z))
        down(lax.rem(z + 1 + n, Z))
        return 0

    lax.fori_loop(0, half - 1, around, 0)
    for d in range(2):
        g_wait(d, half - 1, d)
    down(lax.rem(z + half, Z))

    def o_wait(i, _):
        src = lax.rem(me + NP - i, NP)
        pltpu.make_async_copy(dr.at[src], dr.at[src], o_r.at[i]).wait()
        return 0

    lax.fori_loop(1, NP, o_wait, 0)

    down_f = jnp.concatenate([ds_ref[i:i + 1, :] for i in range(ds_ref.shape[0])], axis=1).astype(F32) * CODE_SCALE

    def total(j, _):
        acc = dr[0, j].astype(F32)
        for q in range(1, NP):
            acc += dr[q, j].astype(F32)
        out_ref[pl.ds(pl.multiple_of(j * ROWS, ROWS), ROWS), :] = (acc * down_f).astype(BF16)
        return 0

    lax.fori_loop(0, Z, total, 0)

    def sent(i, _):
        a_copy(i).wait_send()
        b_copy(i).wait_send()
        pltpu.make_async_copy(dr.at[0], dr.at[0], o_s.at[i]).wait()
        return 0

    lax.fori_loop(1, NP, sent, 0)
    tok_sent()

    def w_sent(ch, _):
        pltpu.make_async_copy(wv.at[ch, a], wv.at[ch, a], w_s.at[ch]).wait()

        @pl.when(diag)
        def _():
            w_forward(ch).wait_send()

        for d in range(2):
            for n in range(half):
                ring_copy(d, ch, n).wait_send()
        return 0

    lax.fori_loop(0, NCH, w_sent, 0)
    pltpu.make_async_copy(dv.at[a], dv.at[a], d_s).wait()

    @pl.when(diag)
    def _():
        d_forward().wait_send()
        for i, ref in enumerate((gs_hbm, us_hbm, sb_hbm)):
            remote(ref, fac.at[i], fac_s.at[i], fac_r.at[i], other_core).wait_send()

    for d in range(2):
        for n in range(half):
            for h in range(2):
                if n < half - 1 or h == d:
                    g_copy(d, n, h).wait_send()


def on_device(Z, K, tokens, gate_codes, up_codes, down_codes, gate_scale, up_scale, down_scale, sign_bits):
    feats = tokens.shape[1]
    width = gate_codes.shape[1]
    NCH = width // BLOCK
    NP = K * YL
    half = Z // 2
    dma = pltpu.SemaphoreType.DMA
    any_spec = pl.BlockSpec(memory_space=pl.ANY)
    vmem_spec = pl.BlockSpec(memory_space=pltpu.VMEM)
    return pl.pallas_call(
        functools.partial(kernel, (Z, K, NCH)),
        out_shape=jax.ShapeDtypeStruct(tokens.shape, BF16),
        in_specs=[any_spec] * 7 + [vmem_spec] * 2,
        out_specs=vmem_spec,
        scratch_shapes=[
            pltpu.VMEM((2, Z, K, ROWS, feats), BF16),
            pltpu.VMEM((NCH, 2, 2, feats, BLOCK), BF16),
            pltpu.VMEM((2, 2, NCH, TILE, feats), BF16),
            pltpu.VMEM((3, 2 * NCH, TILE), jnp.int32),
            pltpu.VMEM((NCH, Z, 2, K * ROWS, BLOCK), BF16),
            pltpu.VMEM((2, NCH, half, 2, K * ROWS, BLOCK), BF16),
            pltpu.VMEM((NCH, 2, K, ROWS, TILE), BF16),
            pltpu.VMEM((NP, NCH, ROWS, TILE), BF16),
            pltpu.VMEM((NP, ROWS, NCH * TILE), BF16),
            pltpu.VMEM((Z, 2, K, ROWS, NCH * TILE), BF16),
            pltpu.VMEM((Z, 2, K, ROWS, feats), BF16),
            pltpu.VMEM((NP, Z, ROWS, feats), BF16),
            dma((2, 5, 2, 2)), dma((2, 5, 2, 2)), dma,
            dma((NCH,)), dma((NCH,)), dma((NCH,)), dma((NCH,)),
            dma, dma, dma, dma,
            dma((3,)), dma((3,)),
            dma((2, NCH, half)), dma((2, NCH, half)),
            dma((NP,)), dma((NP,)), dma((NP,)), dma((NP,)),
            dma((2, half, 2)), dma((2, half, 2)),
            dma((NP,)), dma((NP,)),
        ],
        compiler_params=pltpu.CompilerParams(
            collective_id=0, has_side_effects=True, vmem_limit_bytes=56 * 1024 * 1024),
    )(
        tokens.reshape(Z, ROWS, feats),
        gate_codes,
        up_codes,
        down_codes.reshape(NCH, 2, TILE, down_codes.shape[1]),
        gate_scale.reshape(2 * NCH, TILE),
        up_scale.reshape(2 * NCH, TILE),
        sign_bits.reshape(2 * NCH, TILE),
        down_scale.reshape(feats // TILE, TILE),
        jnp.asarray(walsh(BLOCK), BF16),
    )


def solution(mesh):
    Z = mesh.shape["seq"] // YL
    K = mesh.shape["tensor"] // CORES
    placed = (
        P("tensor", "seq"),
        P("seq", "tensor"),
        P("seq", "tensor"),
        P("tensor", "seq"),
        P("tensor"),
        P("tensor"),
        P("seq"),
        P("tensor"),
    )
    return jax.shard_map(
        functools.partial(on_device, Z, K), mesh=mesh, in_specs=placed, out_specs=P("tensor", "seq"), check_vma=False
    )
```

```python
import functools
import math

import jax
import jax.numpy as jnp
import numpy as np
from jax import lax
from jax.experimental import pallas as pl
from jax.experimental.pallas import tpu as pltpu
from jax.sharding import PartitionSpec as P

BLOCK = 256
TILE = 128
ROWS = 16
YL = 2
YH = 2
CORES = 2
CODE_SCALE = 2.0 ** (-24)
MESH = pl.DeviceIdType.MESH
F32 = jnp.float32
BF16 = jnp.bfloat16


def walsh(extent):
    ids = np.arange(extent)
    common = ids[:, None] & ids[None, :]
    parity = np.zeros_like(common)
    while common.any():
        parity ^= common & 1
        common = common >> 1
    return (1 - 2 * parity).astype(np.float32)


def kernel(
    cfg,
    tok_hbm, gate_hbm, up_hbm, down_hbm, gs_hbm, us_hbm, sb_hbm, ds_ref, walsh_ref,
    out_ref,
    tok, wv, dv, fac, part, ring, lr, ar, br, agr, dp, dr,
    tok_s, tok_r, tok_o, wa, wb, w_s, wf_s, d_a, d_b, d_s, df_s, fac_r, fac_s,
    ring_s, ring_r, a_s, a_r, b_s, b_r, g_s, g_r, o_s, o_r,
):
    Z, K, NCH = cfg
    NP = K * YL
    half = Z // 2
    seq = lax.axis_index("seq")
    ten = lax.axis_index("tensor")
    z = seq // YL
    a = lax.rem(seq, YL)
    k = ten // CORES
    c = lax.rem(ten, CORES)
    me = k * YL + a
    diag = a == c

    def plane(p):
        return (z * YL + lax.rem(p, YL), (p // YL) * CORES + c)

    def ring_dev(d):
        step = 1 if d == 0 else Z - 1
        return (lax.rem(z + step, Z) * YL + a, ten)

    other_core = (seq, k * CORES + (1 - c))
    other_y = (z * YL + (1 - a), ten)

    def remote(src, dst, ss, rs, dev):
        return pltpu.make_async_remote_copy(
            src_ref=src, dst_ref=dst, send_sem=ss, recv_sem=rs,
            device_id=dev, device_id_type=MESH)

    NY = YH * YL
    NX = NP // NY
    x, y = k // YH, lax.rem(k, YH) * YL + a

    def chip(cx, cy):
        return (z * YL + lax.rem(cy, YL), (cx * YH + cy // YL) * CORES + c)

    def moved(axis, by):
        if axis == 0:
            return lax.rem(x + by, NX), y
        return x, lax.rem(y + by, NY)

    barrier = pltpu.get_barrier_semaphore()
    near = [chip(*moved(0, 1)), chip(*moved(0, NX - 1)), chip(*moved(1, 1)), chip(*moved(1, NY - 1)),
            other_core, ring_dev(0), ring_dev(1)]
    for dev in near:
        pl.semaphore_signal(barrier, inc=1, device_id=dev, device_id_type=MESH)
    pl.semaphore_wait(barrier, len(near))

    feats = tok.shape[-1]
    wide = feats // 2
    tok_own = pltpu.make_async_copy(tok_hbm, tok.at[a, :, k], tok_o)

    def spot(f, cx, cy, rows=slice(None)):
        return tok.at[lax.rem(cy, YL), rows, cx * YH + cy // YL, :, f * wide:(f + 1) * wide]

    def tok_copy(f, stage, i, d, hop):
        axis = f if stage == 0 else 1 - f
        size = NX if axis == 0 else NY
        by = 1 if d == 0 else size - 1
        dev = chip(*moved(axis, by))
        back = size - 1 if d == 0 else 1
        cx, cy = moved(axis, back) if hop else (x, y)
        if stage == 1:
            if f == 0:
                cx = lax.rem(x + i, NX)
            else:
                cy = lax.rem(y + i, NY)
        rows = slice(None) if not hop else (slice(0, Z // 2) if d == 0 else slice(Z // 2, Z))
        sem = (f, 1 + i if stage == 1 else 0, d, hop)
        dst = spot(f, cx, cy, rows)
        src = tok_hbm.at[:, :, f * wide:(f + 1) * wide] if stage == 0 and not hop else dst
        if stage == 1 and not hop and i == 0:
            src = tok_hbm.at[:, :, f * wide:(f + 1) * wide]
        return remote(src, dst, tok_s.at[sem], tok_r.at[sem], dev)

    def tok_arrived(f, stage, i, d, hop):
        axis = f if stage == 0 else 1 - f
        size = NX if axis == 0 else NY
        n = 2 if hop else 1
        by = size - n if d == 0 else n
        cx, cy = moved(axis, by)
        if stage == 1:
            if f == 0:
                cx = lax.rem(x + i, NX)
            else:
                cy = lax.rem(y + i, NY)
        rows = slice(None) if not hop else (slice(0, Z // 2) if d == 0 else slice(Z // 2, Z))
        sem = (f, 1 + i if stage == 1 else 0, d, hop)
        ref = spot(f, cx, cy, rows)
        pltpu.make_async_copy(ref, ref, tok_r.at[sem]).wait()

    def tok_begin():
        for f in range(2):
            for d in range(2):
                tok_copy(f, 0, 0, d, 0).start()
        tok_own.start()
        for f in range(2):
            for d in range(2):
                tok_copy(f, 1, 0, d, 0).start()

    def tok_relay():
        for d in range(2):
            for f in range(2):
                tok_arrived(f, 0, 0, d, 0)
                tok_copy(f, 0, 0, d, 1).start()
                i = 3 if d == 0 else 1
                for e in range(2):
                    tok_copy(f, 1, i, e, 0).start()
        for f in range(2):
            for d in range(2):
                tok_arrived(f, 0, 0, d, 1)
            for e in range(2):
                tok_copy(f, 1, 2, e, 0).start()
        for i in (0, 3, 1, 2):
            for f in range(2):
                for d in range(2):
                    tok_arrived(f, 1, i, d, 0)
                    tok_copy(f, 1, i, d, 1).start()
        for i in (0, 3, 1, 2):
            for f in range(2):
                for d in range(2):
                    tok_arrived(f, 1, i, d, 1)
        tok_own.wait()

    def tok_sent():
        for f in range(2):
            for d in range(2):
                for hop in range(2):
                    tok_copy(f, 0, 0, d, hop).wait_send()
                    for i in range(4):
                        tok_copy(f, 1, i, d, hop).wait_send()

    tok_begin()

    def chunk_of(ref, ch):
        return ref.at[:, pl.ds(pl.multiple_of(ch * BLOCK, BLOCK), BLOCK)]

    def w_start(ch):
        for g, ref in enumerate((gate_hbm, up_hbm)):
            src = chunk_of(ref, ch)
            dst = wv.at[ch, a, g]

            @pl.when(diag)
            def _():
                pltpu.make_async_copy(src, dst, wa.at[ch]).start()
                remote(src, dst, w_s.at[ch], wa.at[ch], other_core).start()

            @pl.when(jnp.logical_not(diag))
            def _():
                remote(src, dst, w_s.at[ch], wb.at[ch], other_y).start()

    def w_wait(ch):
        pltpu.make_async_copy(wv.at[ch, a], wv.at[ch, a], wa.at[ch]).wait()
        pltpu.make_async_copy(wv.at[ch, 1 - a], wv.at[ch, 1 - a], wb.at[ch]).wait()

    def w_forward(ch):
        return remote(wv.at[ch, 1 - a], wv.at[ch, 1 - a], wf_s.at[ch], wb.at[ch], other_core)

    def d_start():
        @pl.when(diag)
        def _():
            pltpu.make_async_copy(down_hbm, dv.at[a], d_a).start()
            remote(down_hbm, dv.at[a], d_s, d_a, other_core).start()

        @pl.when(jnp.logical_not(diag))
        def _():
            remote(down_hbm, dv.at[a], d_s, d_b, other_y).start()

    def d_forward():
        return remote(dv.at[1 - a], dv.at[1 - a], df_s, d_b, other_core)

    ahead = min(3, NCH)
    w_start(0)

    @pl.when(diag)
    def _():
        for i, ref in enumerate((gs_hbm, us_hbm, sb_hbm)):
            pltpu.make_async_copy(ref, fac.at[i], fac_r.at[i]).start()
            remote(ref, fac.at[i], fac_s.at[i], fac_r.at[i], other_core).start()

    tok_relay()
    for ch in range(1, ahead):
        w_start(ch)
    for i in range(3):
        pltpu.make_async_copy(fac.at[i], fac.at[i], fac_r.at[i]).wait()

    def ring_copy(d, ch, n):
        step = half - n if d == 0 else Z - half + n
        j = lax.rem(z + step, Z)
        if n == 0:
            return remote(part.at[ch, j, d], ring.at[d, ch, n, d], ring_s.at[d, ch, n], ring_r.at[d, ch, n], ring_dev(d))
        return remote(part.at[ch, j], ring.at[d, ch, n], ring_s.at[d, ch, n], ring_r.at[d, ch, n], ring_dev(d))

    def product(ch):
        w_wait(ch)

        @pl.when(diag)
        def _():
            w_forward(ch).start()

        def rows(m, _):
            for g in range(2):
                acc = jnp.zeros((2 * K * ROWS, BLOCK), F32)
                for f in range(2):
                    x = tok[f, pl.ds(2 * m, 2)].reshape(2 * K * ROWS, -1)
                    acc += jnp.dot(x, wv[ch, f, g], preferred_element_type=F32)
                part[ch, pl.ds(2 * m, 2), g] = acc.astype(BF16).reshape(2, K * ROWS, BLOCK)
            return 0

        lax.fori_loop(0, Z // 2, rows, 0)

        @pl.when(ch + ahead < NCH)
        def _():
            w_start(ch + ahead)

        @pl.when(ch == NCH - 1)
        def _():
            d_start()

    def middle(ch, n):
        for d in range(2):
            ring_copy(d, ch, n - 1).wait_recv()
            step = half - n if d == 0 else Z - half + n
            j = lax.rem(z + step, Z)
            for g in ((d,) if n == 1 else (0, 1)):
                part[ch, j, g] = (part[ch, j, g].astype(F32) + ring[d, ch, n - 1, g].astype(F32)).astype(BF16)
            ring_copy(d, ch, n).start()

    def last(ch):
        n = half - 1
        for d in range(2):
            ring_copy(d, ch, n).wait_recv()
        sums = [
            part[ch, z, g].astype(F32) + ring[0, ch, n, g].astype(F32) + ring[1, ch, n, g].astype(F32)
            for g in range(2)
        ]
        gate_f, up_f, sign = [
            jnp.concatenate([fac[i, pl.ds(2 * ch + h, 1), :] for h in range(2)], axis=1) for i in range(3)
        ]
        gate = sums[0] * (gate_f.astype(F32) * CODE_SCALE)
        up = sums[1] * (up_f.astype(F32) * CODE_SCALE)
        hidden = gate / (1.0 + jnp.exp(-gate)) * up * (2 * sign - 1).astype(F32)
        hi = hidden.astype(BF16)
        lo = (hidden - hi.astype(F32)).astype(BF16)
        w = walsh_ref[...]
        turned = jnp.dot(hi, w, preferred_element_type=F32) + jnp.dot(lo, w, preferred_element_type=F32)
        turned = (turned * (1.0 / math.sqrt(BLOCK))).astype(BF16)
        for h in range(2):
            lr[ch, h] = turned[:, h * TILE:(h + 1) * TILE].reshape(K, ROWS, TILE)

    my_r, my_h = me // 2, lax.rem(me, 2)

    def a_copy(ch, i):
        p = lax.rem(me + i, NP)
        return remote(lr.at[ch, lax.rem(p, 2), p // 2], ar.at[ch, me], a_s.at[ch], a_r.at[ch], plane(p))

    def b_copy(ch, i):
        p = lax.rem(me + i, NP)
        return remote(br.at[ch, p], agr.at[z, ch, my_h, my_r], b_s.at[ch], b_r.at[ch], plane(p))

    def others(copy, ch):
        def start(i, _):
            copy(ch, i).start()
            return 0

        lax.fori_loop(1, NP, start, 0)

    def all_others(sem):
        pltpu.make_async_copy(ar.at[0, 1:NP], ar.at[0, 1:NP], sem).wait()

    def a_send(ch):
        others(a_copy, ch)
        ar[ch, me] = lr[ch, my_h, my_r]

    def mix(ch):
        all_others(a_r.at[ch])
        vals = [ar[ch, q].astype(F32) for q in range(NP)]
        bit = 1
        while bit < NP:
            nxt = list(vals)
            for q in range(NP):
                if not q & bit:
                    nxt[q] = vals[q] + vals[q | bit]
                    nxt[q | bit] = vals[q] - vals[q | bit]
            vals = nxt
            bit *= 2
        for q in range(NP):
            br[ch, q] = (vals[q] * (1.0 / math.sqrt(NP))).astype(BF16)
        others(b_copy, ch)
        agr[z, ch, my_h, my_r] = br[ch, me]

    def g_copy(d, ch, n):
        j = lax.rem(z + (Z - n if d == 0 else n), Z)
        ref = agr.at[j, ch] if n < half - 1 else agr.at[j, ch, d]
        return remote(ref, ref, g_s.at[d, ch, n], g_r.at[d, ch, n], ring_dev(d))

    def g_wait(d, ch, n):
        j = lax.rem(z + (2 * Z - 1 - n if d == 0 else 1 + n), Z)
        ref = agr.at[j, ch] if n < half - 1 else agr.at[j, ch, d]
        pltpu.make_async_copy(ref, ref, g_r.at[d, ch, n]).wait()

    def g_send(ch, n):
        for d in range(2):
            g_copy(d, ch, n).start()

    def g_take(ch, n):
        for d in range(2):
            g_wait(d, ch, n)
            if n + 1 < half:
                g_copy(d, ch, n + 1).start()

    def o_copy(j, i):
        p = lax.rem(me + i, NP)
        return remote(dp.at[j, lax.rem(p, 2), p // 2], dr.at[me, j], o_s.at[i], o_r.at[i], plane(p))

    def down(j):
        x = jnp.concatenate(
            [agr[j, ch, h].reshape(K * ROWS, TILE) for ch in range(NCH) for h in range(2)], axis=1)
        for f in range(2):
            for q in range(feats // BLOCK):
                cols = slice(q * BLOCK, (q + 1) * BLOCK)
                acc = jnp.dot(x, dv[f, :, :, :, cols].reshape(NCH * BLOCK, BLOCK), preferred_element_type=F32)
                dp[j, f, :, :, cols] = acc.astype(BF16).reshape(K, ROWS, BLOCK)

        def o_start(i, _):
            o_copy(j, i).start()
            return 0

        lax.fori_loop(1, NP, o_start, 0)
        dr[me, j] = dp[j, a, k]

    def down_near(n):
        def one(i, _):
            down(lax.rem(z + jnp.where(i == 0, Z - 1 - n, 1 + n), Z))
            return 0

        lax.fori_loop(0, 2 if n < half - 1 else 1, one, 0)

    def slot(t, _):
        def at(n, do):
            ch = t - n

            @pl.when(jnp.logical_and(ch >= 0, ch < NCH))
            def _():
                do(ch)

        def ring_first(ch):
            for d in range(2):
                ring_copy(d, ch, 0).start()

        def back(ch):
            all_others(b_r.at[ch])
            g_send(ch, 0)

        at(0, ring_first)
        for n in range(half - 1, 0, -1):
            at(n, functools.partial(middle, n=n))
        for n in range(half - 1, -1, -1):
            at(half + 3 + n, functools.partial(g_take, n=n))
        at(half + 2, back)
        at(half + 1, mix)
        at(half, last)
        at(half, a_send)
        at(-1, product)

        @pl.when(t == NCH + half - 1)
        def _():
            pltpu.make_async_copy(dv.at[a], dv.at[a], d_a).wait()
            pltpu.make_async_copy(dv.at[1 - a], dv.at[1 - a], d_b).wait()

            @pl.when(diag)
            def _():
                d_forward().start()

        @pl.when(t == NCH - 1 + half + 2)
        def _():
            down(z)

        for n in range(half):
            @pl.when(t == NCH - 1 + half + 3 + n)
            def _():
                down_near(n)

        return 0

    product(0)
    lax.fori_loop(0, NCH + 2 * half + 2, slot, 0)

    def o_wait(i, _):
        src = lax.rem(me + NP - i, NP)
        pltpu.make_async_copy(dr.at[src], dr.at[src], o_r.at[i]).wait()
        return 0

    lax.fori_loop(1, NP, o_wait, 0)

    down_f = jnp.concatenate([ds_ref[i:i + 1, :] for i in range(ds_ref.shape[0])], axis=1).astype(F32) * CODE_SCALE

    def total(j, _):
        acc = dr[0, j].astype(F32)
        for q in range(1, NP):
            acc += dr[q, j].astype(F32)
        out_ref[pl.ds(pl.multiple_of(j * ROWS, ROWS), ROWS), :] = (acc * down_f).astype(BF16)
        return 0

    lax.fori_loop(0, Z, total, 0)

    def sent(i, _):
        pltpu.make_async_copy(dr.at[0], dr.at[0], o_s.at[i]).wait()
        return 0

    lax.fori_loop(1, NP, sent, 0)
    tok_sent()

    def w_sent(ch, _):
        pltpu.make_async_copy(wv.at[ch, a], wv.at[ch, a], w_s.at[ch]).wait()

        @pl.when(diag)
        def _():
            w_forward(ch).wait_send()

        for d in range(2):
            for n in range(half):
                ring_copy(d, ch, n).wait_send()
                g_copy(d, ch, n).wait_send()
        all_others(a_s.at[ch])
        all_others(b_s.at[ch])
        return 0

    lax.fori_loop(0, NCH, w_sent, 0)
    pltpu.make_async_copy(dv.at[a], dv.at[a], d_s).wait()

    @pl.when(diag)
    def _():
        d_forward().wait_send()
        for i, ref in enumerate((gs_hbm, us_hbm, sb_hbm)):
            remote(ref, fac.at[i], fac_s.at[i], fac_r.at[i], other_core).wait_send()


def on_device(Z, K, tokens, gate_codes, up_codes, down_codes, gate_scale, up_scale, down_scale, sign_bits):
    feats = tokens.shape[1]
    width = gate_codes.shape[1]
    NCH = width // BLOCK
    NP = K * YL
    half = Z // 2
    dma = pltpu.SemaphoreType.DMA
    any_spec = pl.BlockSpec(memory_space=pl.ANY)
    vmem_spec = pl.BlockSpec(memory_space=pltpu.VMEM)
    return pl.pallas_call(
        functools.partial(kernel, (Z, K, NCH)),
        out_shape=jax.ShapeDtypeStruct(tokens.shape, BF16),
        in_specs=[any_spec] * 7 + [vmem_spec] * 2,
        out_specs=vmem_spec,
        scratch_shapes=[
            pltpu.VMEM((2, Z, K, ROWS, feats), BF16),
            pltpu.VMEM((NCH, 2, 2, feats, BLOCK), BF16),
            pltpu.VMEM((2, NCH, 2, TILE, feats), BF16),
            pltpu.VMEM((3, 2 * NCH, TILE), jnp.int32),
            pltpu.VMEM((NCH, Z, 2, K * ROWS, BLOCK), BF16),
            pltpu.VMEM((2, NCH, half, 2, K * ROWS, BLOCK), BF16),
            pltpu.VMEM((NCH, 2, K, ROWS, TILE), BF16),
            pltpu.VMEM((NCH, NP, ROWS, TILE), BF16),
            pltpu.VMEM((NCH, NP, ROWS, TILE), BF16),
            pltpu.VMEM((Z, NCH, 2, K, ROWS, TILE), BF16),
            pltpu.VMEM((Z, 2, K, ROWS, feats), BF16),
            pltpu.VMEM((NP, Z, ROWS, feats), BF16),
            dma((2, 5, 2, 2)), dma((2, 5, 2, 2)), dma,
            dma((NCH,)), dma((NCH,)), dma((NCH,)), dma((NCH,)),
            dma, dma, dma, dma,
            dma((3,)), dma((3,)),
            dma((2, NCH, half)), dma((2, NCH, half)),
            dma((NCH,)), dma((NCH,)), dma((NCH,)), dma((NCH,)),
            dma((2, NCH, half)), dma((2, NCH, half)),
            dma((NP,)), dma((NP,)),
        ],
        compiler_params=pltpu.CompilerParams(
            collective_id=0, has_side_effects=True, vmem_limit_bytes=56 * 1024 * 1024),
    )(
        tokens.reshape(Z, ROWS, feats),
        gate_codes,
        up_codes,
        down_codes.reshape(NCH, 2, TILE, down_codes.shape[1]),
        gate_scale.reshape(2 * NCH, TILE),
        up_scale.reshape(2 * NCH, TILE),
        sign_bits.reshape(2 * NCH, TILE),
        down_scale.reshape(feats // TILE, TILE),
        jnp.asarray(walsh(BLOCK), BF16),
    )


def solution(mesh):
    Z = mesh.shape["seq"] // YL
    K = mesh.shape["tensor"] // CORES
    placed = (
        P("tensor", "seq"),
        P("seq", "tensor"),
        P("seq", "tensor"),
        P("tensor", "seq"),
        P("tensor"),
        P("tensor"),
        P("seq"),
        P("tensor"),
    )
    return jax.shard_map(
        functools.partial(on_device, Z, K), mesh=mesh, in_specs=placed, out_specs=P("tensor", "seq"), check_vma=False
    )
```

```python
import functools
import math

import jax
import jax.numpy as jnp
from jax import lax
from jax.experimental import pallas as pl
from jax.experimental.pallas import tpu as pltpu
from jax.sharding import PartitionSpec as P

BLOCK = 256
TILE = 128
ROWS = 16
YL = 2
YH = 2
CORES = 2
CODE_SCALE = 2.0 ** (-24)
MESH = pl.DeviceIdType.MESH
F32 = jnp.float32
BF16 = jnp.bfloat16


def kernel(
    cfg,
    tok_hbm, gate_hbm, up_hbm, down_hbm, gs_hbm, us_hbm, sb_hbm, ds_ref,
    out_ref,
    tok, wv, dv, fac, part, ring, lr, ar, br, agr, dp0, dp1, o1x, o1y, v0, v1, o2x, o2y, wtab,
    tok_s, tok_r, tok_o, wa, wb, w_s, wf_s, d_a, d_b, d_s, df_s, fac_r, fac_s,
    ring_s, ring_r, a_s, a_r, b_s, b_r, g_s, g_r, o_s, o1_r, o2_r,
):
    Z, K, NCH = cfg
    NP = K * YL
    half = Z // 2
    seq = lax.axis_index("seq")
    ten = lax.axis_index("tensor")
    z = seq // YL
    a = lax.rem(seq, YL)
    k = ten // CORES
    c = lax.rem(ten, CORES)
    me = k * YL + a
    diag = a == c

    def plane(p):
        return (z * YL + lax.rem(p, YL), (p // YL) * CORES + c)

    def ring_dev(d):
        step = 1 if d == 0 else Z - 1
        return (lax.rem(z + step, Z) * YL + a, ten)

    other_core = (seq, k * CORES + (1 - c))
    other_y = (z * YL + (1 - a), ten)

    def remote(src, dst, ss, rs, dev):
        return pltpu.make_async_remote_copy(
            src_ref=src, dst_ref=dst, send_sem=ss, recv_sem=rs,
            device_id=dev, device_id_type=MESH)

    NY = YH * YL
    NX = NP // NY
    x, y = k // YH, lax.rem(k, YH) * YL + a

    def chip(cx, cy):
        return (z * YL + lax.rem(cy, YL), (cx * YH + cy // YL) * CORES + c)

    def moved(axis, by):
        if axis == 0:
            return lax.rem(x + by, NX), y
        return x, lax.rem(y + by, NY)

    bits = lax.broadcasted_iota(jnp.int32, (BLOCK, BLOCK), 0) & lax.broadcasted_iota(jnp.int32, (BLOCK, BLOCK), 1)
    for by in (4, 2, 1):
        bits = bits ^ (bits >> by)
    wtab[...] = (1 - 2 * (bits & 1)).astype(F32).astype(BF16)

    barrier = pltpu.get_barrier_semaphore()
    near = [chip(*moved(0, 1)), chip(*moved(0, NX - 1)), chip(*moved(1, 1)), chip(*moved(1, NY - 1)),
            other_core, ring_dev(0), ring_dev(1)]
    for dev in near:
        pl.semaphore_signal(barrier, inc=1, device_id=dev, device_id_type=MESH)
    pl.semaphore_wait(barrier, len(near))

    feats = tok.shape[-1]
    wide = feats // 2
    tok_own = pltpu.make_async_copy(tok_hbm, tok.at[a, :, k], tok_o)

    def spot(f, cx, cy, rows=slice(None)):
        return tok.at[lax.rem(cy, YL), rows, cx * YH + cy // YL, :, f * wide:(f + 1) * wide]

    def tok_copy(f, stage, i, d, hop):
        axis = f if stage == 0 else 1 - f
        size = NX if axis == 0 else NY
        by = 1 if d == 0 else size - 1
        dev = chip(*moved(axis, by))
        back = size - 1 if d == 0 else 1
        cx, cy = moved(axis, back) if hop else (x, y)
        if stage == 1:
            if f == 0:
                cx = lax.rem(x + i, NX)
            else:
                cy = lax.rem(y + i, NY)
        rows = slice(None) if not hop else (slice(0, Z // 2) if d == 0 else slice(Z // 2, Z))
        sem = (f, 1 + i if stage == 1 else 0, d, hop)
        dst = spot(f, cx, cy, rows)
        src = tok_hbm.at[:, :, f * wide:(f + 1) * wide] if stage == 0 and not hop else dst
        if stage == 1 and not hop and i == 0:
            src = tok_hbm.at[:, :, f * wide:(f + 1) * wide]
        return remote(src, dst, tok_s.at[sem], tok_r.at[sem], dev)

    def tok_arrived(f, stage, i, d, hop):
        axis = f if stage == 0 else 1 - f
        size = NX if axis == 0 else NY
        n = 2 if hop else 1
        by = size - n if d == 0 else n
        cx, cy = moved(axis, by)
        if stage == 1:
            if f == 0:
                cx = lax.rem(x + i, NX)
            else:
                cy = lax.rem(y + i, NY)
        rows = slice(None) if not hop else (slice(0, Z // 2) if d == 0 else slice(Z // 2, Z))
        sem = (f, 1 + i if stage == 1 else 0, d, hop)
        ref = spot(f, cx, cy, rows)
        pltpu.make_async_copy(ref, ref, tok_r.at[sem]).wait()

    def tok_begin():
        for f in range(2):
            for d in range(2):
                tok_copy(f, 0, 0, d, 0).start()
        tok_own.start()
        for f in range(2):
            for d in range(2):
                tok_copy(f, 1, 0, d, 0).start()

    def tok_relay():
        for d in range(2):
            for f in range(2):
                tok_arrived(f, 0, 0, d, 0)
                tok_copy(f, 0, 0, d, 1).start()
                i = 3 if d == 0 else 1
                for e in range(2):
                    tok_copy(f, 1, i, e, 0).start()
        for f in range(2):
            for d in range(2):
                tok_arrived(f, 0, 0, d, 1)
            for e in range(2):
                tok_copy(f, 1, 2, e, 0).start()
        for i in (0, 3, 1, 2):
            for f in range(2):
                for d in range(2):
                    tok_arrived(f, 1, i, d, 0)
                    tok_copy(f, 1, i, d, 1).start()
        for i in (0, 3, 1, 2):
            for f in range(2):
                for d in range(2):
                    tok_arrived(f, 1, i, d, 1)
        tok_own.wait()

    def tok_sent():
        for f in range(2):
            for d in range(2):
                for hop in range(2):
                    tok_copy(f, 0, 0, d, hop).wait_send()
                    for i in range(4):
                        tok_copy(f, 1, i, d, hop).wait_send()

    tok_begin()

    def chunk_of(ref, ch):
        return ref.at[:, pl.ds(pl.multiple_of(ch * BLOCK, BLOCK), BLOCK)]

    def w_start(ch):
        for g, ref in enumerate((gate_hbm, up_hbm)):
            src = chunk_of(ref, ch)
            dst = wv.at[ch, a, g]

            @pl.when(diag)
            def _():
                pltpu.make_async_copy(src, dst, wa.at[ch]).start()
                remote(src, dst, w_s.at[ch], wa.at[ch], other_core).start()

            @pl.when(jnp.logical_not(diag))
            def _():
                remote(src, dst, w_s.at[ch], wb.at[ch], other_y).start()

    def w_wait(ch):
        pltpu.make_async_copy(wv.at[ch, a], wv.at[ch, a], wa.at[ch]).wait()
        pltpu.make_async_copy(wv.at[ch, 1 - a], wv.at[ch, 1 - a], wb.at[ch]).wait()

    def w_forward(ch):
        return remote(wv.at[ch, 1 - a], wv.at[ch, 1 - a], wf_s.at[ch], wb.at[ch], other_core)

    def d_start():
        @pl.when(diag)
        def _():
            pltpu.make_async_copy(down_hbm, dv.at[a], d_a).start()
            remote(down_hbm, dv.at[a], d_s, d_a, other_core).start()

        @pl.when(jnp.logical_not(diag))
        def _():
            remote(down_hbm, dv.at[a], d_s, d_b, other_y).start()

    def d_forward():
        return remote(dv.at[1 - a], dv.at[1 - a], df_s, d_b, other_core)

    ahead = min(3, NCH)
    w_start(0)

    @pl.when(diag)
    def _():
        for i, ref in enumerate((gs_hbm, us_hbm, sb_hbm)):
            pltpu.make_async_copy(ref, fac.at[i], fac_r.at[i]).start()
            remote(ref, fac.at[i], fac_s.at[i], fac_r.at[i], other_core).start()

    tok_relay()
    for ch in range(1, ahead):
        w_start(ch)
    for i in range(3):
        pltpu.make_async_copy(fac.at[i], fac.at[i], fac_r.at[i]).wait()

    def ring_copy(d, ch, n):
        step = half - n if d == 0 else Z - half + n
        j = lax.rem(z + step, Z)
        if n == 0:
            return remote(part.at[ch, j, d], ring.at[d, ch, n, d], ring_s.at[d, ch, n], ring_r.at[d, ch, n], ring_dev(d))
        return remote(part.at[ch, j], ring.at[d, ch, n], ring_s.at[d, ch, n], ring_r.at[d, ch, n], ring_dev(d))

    def product(ch):
        w_wait(ch)

        @pl.when(diag)
        def _():
            w_forward(ch).start()

        def rows(m, _):
            for g in range(2):
                acc = jnp.zeros((2 * K * ROWS, BLOCK), F32)
                for f in range(2):
                    x = tok[f, pl.ds(2 * m, 2)].reshape(2 * K * ROWS, -1)
                    acc += jnp.dot(x, wv[ch, f, g], preferred_element_type=F32)
                part[ch, pl.ds(2 * m, 2), g] = acc.astype(BF16).reshape(2, K * ROWS, BLOCK)
            return 0

        lax.fori_loop(0, Z // 2, rows, 0)

        @pl.when(ch + ahead < NCH)
        def _():
            w_start(ch + ahead)

        @pl.when(ch == NCH - 1)
        def _():
            d_start()

    def middle(ch, n):
        for d in range(2):
            ring_copy(d, ch, n - 1).wait_recv()
            step = half - n if d == 0 else Z - half + n
            j = lax.rem(z + step, Z)
            for g in ((d,) if n == 1 else (0, 1)):
                part[ch, j, g] = (part[ch, j, g].astype(F32) + ring[d, ch, n - 1, g].astype(F32)).astype(BF16)
            ring_copy(d, ch, n).start()

    def last(ch):
        n = half - 1
        for d in range(2):
            ring_copy(d, ch, n).wait_recv()
        sums = [
            part[ch, z, g].astype(F32) + ring[0, ch, n, g].astype(F32) + ring[1, ch, n, g].astype(F32)
            for g in range(2)
        ]
        gate_f, up_f, sign = [
            jnp.concatenate([fac[i, pl.ds(2 * ch + h, 1), :] for h in range(2)], axis=1) for i in range(3)
        ]
        gate = sums[0] * (gate_f.astype(F32) * CODE_SCALE)
        up = sums[1] * (up_f.astype(F32) * CODE_SCALE)
        hidden = gate / (1.0 + jnp.exp(-gate)) * up * (2 * sign - 1).astype(F32)
        hi = hidden.astype(BF16)
        lo = (hidden - hi.astype(F32)).astype(BF16)
        w = wtab[...]
        turned = jnp.dot(hi, w, preferred_element_type=F32) + jnp.dot(lo, w, preferred_element_type=F32)
        turned = (turned * (1.0 / math.sqrt(BLOCK))).astype(BF16)
        for h in range(2):
            lr[ch, h] = turned[:, h * TILE:(h + 1) * TILE].reshape(K, ROWS, TILE)

    my_r, my_h = me // 2, lax.rem(me, 2)

    def a_copy(ch, i):
        p = lax.rem(me + i, NP)
        return remote(lr.at[ch, lax.rem(p, 2), p // 2], ar.at[ch, me], a_s.at[ch], a_r.at[ch], plane(p))

    def b_copy(ch, i):
        p = lax.rem(me + i, NP)
        return remote(br.at[ch, p], agr.at[z, ch, my_h, my_r], b_s.at[ch], b_r.at[ch], plane(p))

    def others(copy, ch):
        def start(i, _):
            copy(ch, i).start()
            return 0

        lax.fori_loop(1, NP, start, 0)

    def all_others(sem):
        pltpu.make_async_copy(ar.at[0, 1:NP], ar.at[0, 1:NP], sem).wait()

    def a_send(ch):
        others(a_copy, ch)
        ar[ch, me] = lr[ch, my_h, my_r]

    def mix(ch):
        all_others(a_r.at[ch])
        vals = [ar[ch, q].astype(F32) for q in range(NP)]
        bit = 1
        while bit < NP:
            nxt = list(vals)
            for q in range(NP):
                if not q & bit:
                    nxt[q] = vals[q] + vals[q | bit]
                    nxt[q | bit] = vals[q] - vals[q | bit]
            vals = nxt
            bit *= 2
        for q in range(NP):
            br[ch, q] = (vals[q] * (1.0 / math.sqrt(NP))).astype(BF16)
        others(b_copy, ch)
        agr[z, ch, my_h, my_r] = br[ch, me]

    def g_copy(d, ch, n):
        j = lax.rem(z + (Z - n if d == 0 else n), Z)
        ref = agr.at[j, ch] if n < half - 1 else agr.at[j, ch, d]
        return remote(ref, ref, g_s.at[d, ch, n], g_r.at[d, ch, n], ring_dev(d))

    def g_wait(d, ch, n):
        j = lax.rem(z + (2 * Z - 1 - n if d == 0 else 1 + n), Z)
        ref = agr.at[j, ch] if n < half - 1 else agr.at[j, ch, d]
        pltpu.make_async_copy(ref, ref, g_r.at[d, ch, n]).wait()

    def g_send(ch, n):
        for d in range(2):
            g_copy(d, ch, n).start()

    def g_take(ch, n):
        for d in range(2):
            g_wait(d, ch, n)
            if n + 1 < half:
                g_copy(d, ch, n + 1).start()

    here = (x, y)
    sizes = (NX, NY)
    quarter = feats // 2

    def o_copy(f, stage, j, i):
        axis = f if stage == 0 else 1 - f
        p = lax.rem(here[axis] + i, sizes[axis])
        dev = chip(p, y) if axis == 0 else chip(x, p)
        if stage == 0:
            return remote((dp0, dp1)[f].at[j, p], (o1x, o1y)[f].at[j, here[axis]], o_s.at[f, 0], o1_r.at[f, j], dev)
        return remote((v0, v1)[f].at[j, p], (o2x, o2y)[f].at[j, here[axis]], o_s.at[f, 1], o2_r.at[f], dev)

    def down(j):
        x_all = jnp.concatenate(
            [agr[j, ch, h].reshape(K * ROWS, TILE) for ch in range(NCH) for h in range(2)], axis=1)
        for f in range(2):
            for e in range(2):
                cols = slice(f * quarter, (f + 1) * quarter)
                acc = jnp.dot(x_all, dv[e, :, :, :, cols].reshape(NCH * BLOCK, quarter), preferred_element_type=F32)
                acc = acc.astype(BF16).reshape(NX, YH, ROWS, quarter)
                for yh in range(YH):
                    if f == 0:
                        dp0[j, :, yh * YL + e] = acc[:, yh]
                    else:
                        dp1[j, yh * YL + e] = acc[:, yh]
            for i in range(1, sizes[f]):
                o_copy(f, 0, j, i).start()
        o1x[j, x] = dp0[j, x]
        o1y[j, y] = dp1[j, y]

    def second(j):
        for f in range(2):
            src = (o1x, o1y)[f]
            got = src.at[j, 1:sizes[f]]
            pltpu.make_async_copy(got, got, o1_r.at[f, j]).wait()
            acc = src[j, 0].astype(F32)
            for q in range(1, sizes[f]):
                acc += src[j, q].astype(F32)
            dst = (v0, v1)[f]
            dst[j] = acc.astype(BF16)
            for i in range(1, sizes[1 - f]):
                o_copy(f, 1, j, i).start()
        o2x[j, y] = v0[j, y]
        o2y[j, x] = v1[j, x]

    def near(do, n):
        def one(i, _):
            do(lax.rem(z + jnp.where(i == 0, Z - 1 - n, 1 + n), Z))
            return 0

        lax.fori_loop(0, 2 if n < half - 1 else 1, one, 0)

    final = NCH - 1 + half + 2

    def slot(t, _):
        def at(n, do):
            ch = t - n

            @pl.when(jnp.logical_and(ch >= 0, ch < NCH))
            def _():
                do(ch)

        def ring_first(ch):
            for d in range(2):
                ring_copy(d, ch, 0).start()

        def back(ch):
            all_others(b_r.at[ch])
            g_send(ch, 0)

        at(0, ring_first)
        for n in range(half - 1, 0, -1):
            at(n, functools.partial(middle, n=n))
        for n in range(half, -1, -1):
            m = final + n - t
            for ch in (NCH - 1 - 2 * m, NCH - 2 * m):
                @pl.when(jnp.logical_and(ch >= 0, ch < NCH))
                def _():
                    if n > 0:
                        g_take(ch, n - 1)
                    else:
                        back(ch)

        at(half + 1, mix)
        at(half, last)
        at(half, a_send)
        at(-1, product)

        @pl.when(t == NCH + half - 1)
        def _():
            pltpu.make_async_copy(dv.at[a], dv.at[a], d_a).wait()
            pltpu.make_async_copy(dv.at[1 - a], dv.at[1 - a], d_b).wait()

            @pl.when(diag)
            def _():
                d_forward().start()

        @pl.when(t == final)
        def _():
            down(z)

        for n in range(half):
            @pl.when(t == final + 1 + n)
            def _():
                if n == 0:
                    second(z)
                else:
                    near(second, n - 1)
                near(down, n)

        return 0

    product(0)
    lax.fori_loop(0, final + half + 1, slot, 0)
    near(second, half - 1)

    for f in range(2):
        got = (o2x, o2y)[f].at[:, 1:sizes[1 - f]]
        pltpu.make_async_copy(got, got, o2_r.at[f]).wait()

    def total(j, _):
        for f in range(2):
            src = (o2x, o2y)[f]
            acc = src[j, 0].astype(F32)
            for q in range(1, sizes[1 - f]):
                acc += src[j, q].astype(F32)
            per = quarter // TILE
            scale = jnp.concatenate([ds_ref[f * per + i:f * per + i + 1, :] for i in range(per)], axis=1)
            out_ref[pl.ds(pl.multiple_of(j * ROWS, ROWS), ROWS), f * quarter:(f + 1) * quarter] = (
                acc * (scale.astype(F32) * CODE_SCALE)).astype(BF16)
        return 0

    lax.fori_loop(0, Z, total, 0)

    for f in range(2):
        for i, out in enumerate(((o1x, o1y)[f].at[:, 1:sizes[f]], (o2x, o2y)[f].at[:, 1:sizes[1 - f]])):
            pltpu.make_async_copy(out, out, o_s.at[f, i]).wait()
    tok_sent()

    def w_sent(ch, _):
        pltpu.make_async_copy(wv.at[ch, a], wv.at[ch, a], w_s.at[ch]).wait()

        @pl.when(diag)
        def _():
            w_forward(ch).wait_send()

        for d in range(2):
            for n in range(half):
                ring_copy(d, ch, n).wait_send()
                g_copy(d, ch, n).wait_send()
        all_others(a_s.at[ch])
        all_others(b_s.at[ch])
        return 0

    lax.fori_loop(0, NCH, w_sent, 0)
    pltpu.make_async_copy(dv.at[a], dv.at[a], d_s).wait()

    @pl.when(diag)
    def _():
        d_forward().wait_send()
        for i, ref in enumerate((gs_hbm, us_hbm, sb_hbm)):
            remote(ref, fac.at[i], fac_s.at[i], fac_r.at[i], other_core).wait_send()


def on_device(Z, K, tokens, gate_codes, up_codes, down_codes, gate_scale, up_scale, down_scale, sign_bits):
    feats = tokens.shape[1]
    width = gate_codes.shape[1]
    NCH = width // BLOCK
    NP = K * YL
    half = Z // 2
    NY = YH * YL
    NX = NP // NY
    dma = pltpu.SemaphoreType.DMA
    any_spec = pl.BlockSpec(memory_space=pl.ANY)
    vmem_spec = pl.BlockSpec(memory_space=pltpu.VMEM)
    return pl.pallas_call(
        functools.partial(kernel, (Z, K, NCH)),
        out_shape=jax.ShapeDtypeStruct(tokens.shape, BF16),
        in_specs=[any_spec] * 7 + [vmem_spec],
        out_specs=vmem_spec,
        scratch_shapes=[
            pltpu.VMEM((2, Z, K, ROWS, feats), BF16),
            pltpu.VMEM((NCH, 2, 2, feats, BLOCK), BF16),
            pltpu.VMEM((2, NCH, 2, TILE, feats), BF16),
            pltpu.VMEM((3, 2 * NCH, TILE), jnp.int32),
            pltpu.VMEM((NCH, Z, 2, K * ROWS, BLOCK), BF16),
            pltpu.VMEM((2, NCH, half, 2, K * ROWS, BLOCK), BF16),
            pltpu.VMEM((NCH, 2, K, ROWS, TILE), BF16),
            pltpu.VMEM((NCH, NP, ROWS, TILE), BF16),
            pltpu.VMEM((NCH, NP, ROWS, TILE), BF16),
            pltpu.VMEM((Z, NCH, 2, K, ROWS, TILE), BF16),
            pltpu.VMEM((Z, NX, NY, ROWS, feats // 2), BF16),
            pltpu.VMEM((Z, NY, NX, ROWS, feats // 2), BF16),
            pltpu.VMEM((Z, NX, NY, ROWS, feats // 2), BF16),
            pltpu.VMEM((Z, NY, NX, ROWS, feats // 2), BF16),
            pltpu.VMEM((Z, NY, ROWS, feats // 2), BF16),
            pltpu.VMEM((Z, NX, ROWS, feats // 2), BF16),
            pltpu.VMEM((Z, NY, ROWS, feats // 2), BF16),
            pltpu.VMEM((Z, NX, ROWS, feats // 2), BF16),
            pltpu.VMEM((BLOCK, BLOCK), BF16),
            dma((2, 5, 2, 2)), dma((2, 5, 2, 2)), dma,
            dma((NCH,)), dma((NCH,)), dma((NCH,)), dma((NCH,)),
            dma, dma, dma, dma,
            dma((3,)), dma((3,)),
            dma((2, NCH, half)), dma((2, NCH, half)),
            dma((NCH,)), dma((NCH,)), dma((NCH,)), dma((NCH,)),
            dma((2, NCH, half)), dma((2, NCH, half)),
            dma((2, 2)), dma((2, Z)), dma((2,)),
        ],
        compiler_params=pltpu.CompilerParams(
            collective_id=0, has_side_effects=True, vmem_limit_bytes=56 * 1024 * 1024),
    )(
        tokens.reshape(Z, ROWS, feats),
        gate_codes,
        up_codes,
        down_codes.reshape(NCH, 2, TILE, down_codes.shape[1]),
        gate_scale.reshape(2 * NCH, TILE),
        up_scale.reshape(2 * NCH, TILE),
        sign_bits.reshape(2 * NCH, TILE),
        down_scale.reshape(feats // TILE, TILE),
    )


def solution(mesh):
    Z = mesh.shape["seq"] // YL
    K = mesh.shape["tensor"] // CORES
    placed = (
        P("tensor", "seq"),
        P("seq", "tensor"),
        P("seq", "tensor"),
        P("tensor", "seq"),
        P("tensor"),
        P("tensor"),
        P("seq"),
        P("tensor"),
    )
    return jax.shard_map(
        functools.partial(on_device, Z, K), mesh=mesh, in_specs=placed, out_specs=P("tensor", "seq"), check_vma=False
    )
```

```python
import functools
import math

import jax
import jax.numpy as jnp
from jax import lax
from jax.experimental import pallas as pl
from jax.experimental.pallas import tpu as pltpu
from jax.sharding import PartitionSpec as P

BLOCK = 256
TILE = 128
ROWS = 16
YL = 2
YH = 2
CORES = 2
CODE_SCALE = 2.0 ** (-24)
MESH = pl.DeviceIdType.MESH
F32 = jnp.float32
BF16 = jnp.bfloat16


def kernel(
    cfg,
    tok_hbm, gate_hbm, up_hbm, down_hbm, gs_hbm, us_hbm, sb_hbm, ds_ref,
    out_ref,
    tok, wv, dv, fac, part, ring, lr, ar, br, agr, dp0, dp1, o1x, o1y, v0, v1, o2x, o2y, wtab,
    tok_s, tok_r, tok_o, wa, wb, w_s, wf_s, d_a, d_b, d_s, df_s, fac_r, fac_s,
    ring_s, ring_r, a_s, a_r, b_s, b_r, g_s, g_r, o_s, o1_r, o2_r,
):
    Z, K, NCH = cfg
    NP = K * YL
    half = Z // 2
    seq = lax.axis_index("seq")
    ten = lax.axis_index("tensor")
    z = seq // YL
    a = lax.rem(seq, YL)
    k = ten // CORES
    c = lax.rem(ten, CORES)
    me = k * YL + a
    diag = a == c

    def plane(p):
        return (z * YL + lax.rem(p, YL), (p // YL) * CORES + c)

    def ring_dev(d):
        step = 1 if d == 0 else Z - 1
        return (lax.rem(z + step, Z) * YL + a, ten)

    other_core = (seq, k * CORES + (1 - c))
    other_y = (z * YL + (1 - a), ten)

    def remote(src, dst, ss, rs, dev):
        return pltpu.make_async_remote_copy(
            src_ref=src, dst_ref=dst, send_sem=ss, recv_sem=rs,
            device_id=dev, device_id_type=MESH)

    NY = YH * YL
    NX = NP // NY
    x, y = k // YH, lax.rem(k, YH) * YL + a

    def chip(cx, cy):
        return (z * YL + lax.rem(cy, YL), (cx * YH + cy // YL) * CORES + c)

    def moved(axis, by):
        if axis == 0:
            return lax.rem(x + by, NX), y
        return x, lax.rem(y + by, NY)

    far = sorted(range(Z), key=lambda step: abs(step - half))
    place = {step: r for r, step in enumerate(far)}
    feats = down_hbm.shape[-1]
    wide = feats // 2

    def tok_own(f, r):
        return pltpu.make_async_copy(
            tok_hbm.at[lax.rem(z + far[r], Z), :, f * wide:(f + 1) * wide], tok.at[a, f, x, y // YL, r], tok_o.at[f, r])

    for f in range(2):
        for r in range(Z):
            tok_own(f, r).start()

    bits = lax.broadcasted_iota(jnp.int32, (BLOCK, BLOCK), 0) & lax.broadcasted_iota(jnp.int32, (BLOCK, BLOCK), 1)
    for by in (4, 2, 1):
        bits = bits ^ (bits >> by)
    wtab[...] = (1 - 2 * (bits & 1)).astype(F32).astype(BF16)

    barrier = pltpu.get_barrier_semaphore()
    peers = [chip(*moved(0, i)) for i in range(1, NX)] + [chip(*moved(1, i)) for i in range(1, NY)]
    peers += [other_core, ring_dev(0), ring_dev(1)]
    for dev in peers:
        pl.semaphore_signal(barrier, inc=1, device_id=dev, device_id_type=MESH)
    for f in range(2):
        for r in range(Z):
            tok_own(f, r).wait()
    pl.semaphore_wait(barrier, len(peers))

    here = (x, y)
    sizes = (NX, NY)
    some = Z // 2

    def tok_copy(piece, f, stage, i, source=False):
        rows = pl.ds(piece * some, some)
        axis = f if stage == 0 else 1 - f
        by = sizes[axis] - i if source else i
        cx, cy = moved(axis, by)
        dev = chip(cx, cy)
        if not source:
            cx, cy = x, y
        if stage == 0:
            ref = tok.at[lax.rem(cy, YL), f, cx, cy // YL, rows]
        elif f == 0:
            ref = tok.at[lax.rem(cy, YL), f, :, cy // YL, rows]
        else:
            ref = tok.at[:, f, cx, :, rows]
        sem = (piece, f, stage, i)
        return remote(ref, ref, tok_s.at[sem], tok_r.at[sem], dev)

    def tok_each(do, piece, stage):
        for i in (1, 3, 2):
            for f in range(2):
                if i < sizes[f if stage == 0 else 1 - f]:
                    do(piece, f, stage, i)

    def tok_send(piece, stage):
        tok_each(lambda *at: tok_copy(*at).start(), piece, stage)

    def tok_take(piece, stage):
        tok_each(lambda *at: tok_copy(*at, source=True).wait_recv(), piece, stage)

    def tok_sent():
        for piece in range(2):
            for stage in range(2):
                tok_each(lambda *at: tok_copy(*at).wait_send(), piece, stage)

    tok_send(0, 0)
    tok_send(1, 0)

    def chunk_of(ref, ch):
        return ref.at[:, pl.ds(pl.multiple_of(ch * BLOCK, BLOCK), BLOCK)]

    def w_start(ch):
        for g, ref in enumerate((gate_hbm, up_hbm)):
            src = chunk_of(ref, ch)
            dst = wv.at[ch, a, g]

            @pl.when(diag)
            def _():
                pltpu.make_async_copy(src, dst, wa.at[ch]).start()
                remote(src, dst, w_s.at[ch], wa.at[ch], other_core).start()

            @pl.when(jnp.logical_not(diag))
            def _():
                remote(src, dst, w_s.at[ch], wb.at[ch], other_y).start()

    def w_wait(ch):
        pltpu.make_async_copy(wv.at[ch, a], wv.at[ch, a], wa.at[ch]).wait()
        pltpu.make_async_copy(wv.at[ch, 1 - a], wv.at[ch, 1 - a], wb.at[ch]).wait()

    def w_forward(ch):
        return remote(wv.at[ch, 1 - a], wv.at[ch, 1 - a], wf_s.at[ch], wb.at[ch], other_core)

    def d_start():
        @pl.when(diag)
        def _():
            pltpu.make_async_copy(down_hbm, dv.at[a], d_a).start()
            remote(down_hbm, dv.at[a], d_s, d_a, other_core).start()

        @pl.when(jnp.logical_not(diag))
        def _():
            remote(down_hbm, dv.at[a], d_s, d_b, other_y).start()

    def d_forward():
        return remote(dv.at[1 - a], dv.at[1 - a], df_s, d_b, other_core)

    ahead = min(3, NCH)
    w_start(0)

    @pl.when(diag)
    def _():
        for i, ref in enumerate((gs_hbm, us_hbm, sb_hbm)):
            pltpu.make_async_copy(ref, fac.at[i], fac_r.at[i]).start()
            remote(ref, fac.at[i], fac_s.at[i], fac_r.at[i], other_core).start()

    for piece in range(2):
        tok_take(piece, 0)
        tok_send(piece, 1)
    tok_take(0, 1)
    for ch in range(1, ahead):
        w_start(ch)
    for i in range(3):
        pltpu.make_async_copy(fac.at[i], fac.at[i], fac_r.at[i]).wait()

    def ring_copy(d, ch, n):
        j = place[half - n if d == 0 else Z - half + n]
        if n == 0:
            return remote(part.at[ch, j, d], ring.at[d, ch, n, d], ring_s.at[d, ch, n], ring_r.at[d, ch, n], ring_dev(d))
        return remote(part.at[ch, j], ring.at[d, ch, n], ring_s.at[d, ch, n], ring_r.at[d, ch, n], ring_dev(d))

    def product_rows(ch, lo, hi):
        def rows(m, _):
            for g in range(2):
                acc = jnp.zeros((2 * K * ROWS, BLOCK), F32)
                for f in range(2):
                    for q in range(2):
                        xs = [tok[f, q, :, :, 2 * m + e].reshape(K * ROWS, wide) for e in range(2)]
                        acc += jnp.dot(jnp.concatenate(xs, axis=0), wv[ch, f, g, q * wide:(q + 1) * wide],
                                       preferred_element_type=F32)
                part[ch, pl.ds(2 * m, 2), g] = acc.astype(BF16).reshape(2, K * ROWS, BLOCK)
            return 0

        lax.fori_loop(lo // 2, hi // 2, rows, 0)

    def w_take(ch):
        w_wait(ch)

        @pl.when(diag)
        def _():
            w_forward(ch).start()

    def w_next(ch):
        @pl.when(ch + ahead < NCH)
        def _():
            w_start(ch + ahead)

        @pl.when(ch == NCH - 1)
        def _():
            d_start()

    def product(ch):
        w_take(ch)
        product_rows(ch, 0, Z)
        w_next(ch)

    def ring_first(ch):
        for d in range(2):
            ring_copy(d, ch, 0).start()

    def middle(ch, n):
        for d in range(2):
            ring_copy(d, ch, n - 1).wait_recv()
            j = place[half - n if d == 0 else Z - half + n]
            for g in ((d,) if n == 1 else (0, 1)):
                part[ch, j, g] = (part[ch, j, g].astype(F32) + ring[d, ch, n - 1, g].astype(F32)).astype(BF16)
            ring_copy(d, ch, n).start()

    def last(ch):
        n = half - 1
        for d in range(2):
            ring_copy(d, ch, n).wait_recv()
        sums = [
            part[ch, place[0], g].astype(F32) + ring[0, ch, n, g].astype(F32) + ring[1, ch, n, g].astype(F32)
            for g in range(2)
        ]
        gate_f, up_f, sign = [
            jnp.concatenate([fac[i, pl.ds(2 * ch + h, 1), :] for h in range(2)], axis=1) for i in range(3)
        ]
        gate = sums[0] * (gate_f.astype(F32) * CODE_SCALE)
        up = sums[1] * (up_f.astype(F32) * CODE_SCALE)
        hidden = gate / (1.0 + jnp.exp(-gate)) * up * (2 * sign - 1).astype(F32)
        hi = hidden.astype(BF16)
        lo = (hidden - hi.astype(F32)).astype(BF16)
        w = wtab[...]
        turned = jnp.dot(hi, w, preferred_element_type=F32) + jnp.dot(lo, w, preferred_element_type=F32)
        turned = (turned * (1.0 / math.sqrt(BLOCK))).astype(BF16)
        for h in range(2):
            lr[ch, h] = turned[:, h * TILE:(h + 1) * TILE].reshape(K, ROWS, TILE)

    my_r, my_h = me // 2, lax.rem(me, 2)

    def a_copy(ch, i):
        p = lax.rem(me + i, NP)
        return remote(lr.at[ch, lax.rem(p, 2), p // 2], ar.at[ch, me], a_s.at[ch], a_r.at[ch], plane(p))

    def b_copy(ch, i):
        p = lax.rem(me + i, NP)
        return remote(br.at[ch, p], agr.at[z, ch, my_h, my_r], b_s.at[ch], b_r.at[ch], plane(p))

    def others(copy, ch):
        def start(i, _):
            copy(ch, i).start()
            return 0

        lax.fori_loop(1, NP, start, 0)

    def all_others(sem):
        pltpu.make_async_copy(ar.at[0, 1:NP], ar.at[0, 1:NP], sem).wait()

    def a_send(ch):
        others(a_copy, ch)
        ar[ch, me] = lr[ch, my_h, my_r]

    def mix(ch):
        all_others(a_r.at[ch])
        vals = [ar[ch, q].astype(F32) for q in range(NP)]
        bit = 1
        while bit < NP:
            nxt = list(vals)
            for q in range(NP):
                if not q & bit:
                    nxt[q] = vals[q] + vals[q | bit]
                    nxt[q | bit] = vals[q] - vals[q | bit]
            vals = nxt
            bit *= 2
        for q in range(NP):
            br[ch, q] = (vals[q] * (1.0 / math.sqrt(NP))).astype(BF16)
        others(b_copy, ch)
        agr[z, ch, my_h, my_r] = br[ch, me]

    def g_copy(d, ch, n):
        j = lax.rem(z + (Z - n if d == 0 else n), Z)
        ref = agr.at[j, ch] if n < half - 1 else agr.at[j, ch, d]
        return remote(ref, ref, g_s.at[d, ch, n], g_r.at[d, ch, n], ring_dev(d))

    def g_wait(d, ch, n):
        j = lax.rem(z + (2 * Z - 1 - n if d == 0 else 1 + n), Z)
        ref = agr.at[j, ch] if n < half - 1 else agr.at[j, ch, d]
        pltpu.make_async_copy(ref, ref, g_r.at[d, ch, n]).wait()

    def g_send(ch, n):
        for d in range(2):
            g_copy(d, ch, n).start()

    def g_take(ch, n):
        for d in range(2):
            g_wait(d, ch, n)
            if n + 1 < half:
                g_copy(d, ch, n + 1).start()

    quarter = wide

    def o_copy(f, stage, j, i):
        axis = f if stage == 0 else 1 - f
        p = lax.rem(here[axis] + i, sizes[axis])
        dev = chip(p, y) if axis == 0 else chip(x, p)
        if stage == 0:
            return remote((dp0, dp1)[f].at[j, p], (o1x, o1y)[f].at[j, here[axis]], o_s.at[f, 0], o1_r.at[f, j], dev)
        return remote((v0, v1)[f].at[j, p], (o2x, o2y)[f].at[j, here[axis]], o_s.at[f, 1], o2_r.at[f], dev)

    def down(j):
        x_all = jnp.concatenate(
            [agr[j, ch, h].reshape(K * ROWS, TILE) for ch in range(NCH) for h in range(2)], axis=1)
        for f in range(2):
            for e in range(2):
                cols = slice(f * quarter, (f + 1) * quarter)
                acc = jnp.dot(x_all, dv[e, :, :, :, cols].reshape(NCH * BLOCK, quarter), preferred_element_type=F32)
                acc = acc.astype(BF16).reshape(NX, YH, ROWS, quarter)
                for yh in range(YH):
                    if f == 0:
                        dp0[j, :, yh * YL + e] = acc[:, yh]
                    else:
                        dp1[j, yh * YL + e] = acc[:, yh]
            for i in range(1, sizes[f]):
                o_copy(f, 0, j, i).start()
        o1x[j, x] = dp0[j, x]
        o1y[j, y] = dp1[j, y]

    def second(j):
        for f in range(2):
            src = (o1x, o1y)[f]
            got = src.at[j, 1:sizes[f]]
            pltpu.make_async_copy(got, got, o1_r.at[f, j]).wait()
            acc = src[j, 0].astype(F32)
            for q in range(1, sizes[f]):
                acc += src[j, q].astype(F32)
            dst = (v0, v1)[f]
            dst[j] = acc.astype(BF16)
            for i in range(1, sizes[1 - f]):
                o_copy(f, 1, j, i).start()
        o2x[j, y] = v0[j, y]
        o2y[j, x] = v1[j, x]

    def near(do, n):
        def one(i, _):
            do(lax.rem(z + jnp.where(i == 0, Z - 1 - n, 1 + n), Z))
            return 0

        lax.fori_loop(0, 2 if n < half - 1 else 1, one, 0)

    final = NCH - 1 + half + 2

    def slot(t, _):
        def at(n, do):
            ch = t - n

            @pl.when(jnp.logical_and(ch >= 0, ch < NCH))
            def _():
                do(ch)

        def back(ch):
            all_others(b_r.at[ch])
            g_send(ch, 0)

        at(0, ring_first)
        for n in range(half - 1, 0, -1):
            at(n, functools.partial(middle, n=n))
        for n in range(half, -1, -1):
            at(half + 2 + n, functools.partial(g_take, n=n - 1) if n else back)
        at(half + 1, mix)
        at(half, last)
        at(half, a_send)
        at(-1, product)

        @pl.when(t == NCH + half - 1)
        def _():
            pltpu.make_async_copy(dv.at[a], dv.at[a], d_a).wait()
            pltpu.make_async_copy(dv.at[1 - a], dv.at[1 - a], d_b).wait()

            @pl.when(diag)
            def _():
                d_forward().start()

        @pl.when(t == final)
        def _():
            down(z)

        for n in range(half):
            @pl.when(t == final + 1 + n)
            def _():
                near(down, n)
                if n == 0:
                    second(z)
                else:
                    near(second, n - 1)

        return 0

    w_take(0)
    product_rows(0, 0, some)
    ring_first(0)
    tok_take(1, 1)
    product_rows(0, some, Z)
    w_next(0)
    product(1)
    lax.fori_loop(1, final + half + 1, slot, 0)
    near(second, half - 1)

    for f in range(2):
        got = (o2x, o2y)[f].at[:, 1:sizes[1 - f]]
        pltpu.make_async_copy(got, got, o2_r.at[f]).wait()

    def total(j, _):
        for f in range(2):
            src = (o2x, o2y)[f]
            acc = src[j, 0].astype(F32)
            for q in range(1, sizes[1 - f]):
                acc += src[j, q].astype(F32)
            per = quarter // TILE
            scale = jnp.concatenate([ds_ref[f * per + i:f * per + i + 1, :] for i in range(per)], axis=1)
            out_ref[pl.ds(pl.multiple_of(j * ROWS, ROWS), ROWS), f * quarter:(f + 1) * quarter] = (
                acc * (scale.astype(F32) * CODE_SCALE)).astype(BF16)
        return 0

    lax.fori_loop(0, Z, total, 0)

    for f in range(2):
        for i, out in enumerate(((o1x, o1y)[f].at[:, 1:sizes[f]], (o2x, o2y)[f].at[:, 1:sizes[1 - f]])):
            pltpu.make_async_copy(out, out, o_s.at[f, i]).wait()
    tok_sent()

    def w_sent(ch, _):
        pltpu.make_async_copy(wv.at[ch, a], wv.at[ch, a], w_s.at[ch]).wait()

        @pl.when(diag)
        def _():
            w_forward(ch).wait_send()

        for d in range(2):
            for n in range(half):
                ring_copy(d, ch, n).wait_send()
                g_copy(d, ch, n).wait_send()
        all_others(a_s.at[ch])
        all_others(b_s.at[ch])
        return 0

    lax.fori_loop(0, NCH, w_sent, 0)
    pltpu.make_async_copy(dv.at[a], dv.at[a], d_s).wait()

    @pl.when(diag)
    def _():
        d_forward().wait_send()
        for i, ref in enumerate((gs_hbm, us_hbm, sb_hbm)):
            remote(ref, fac.at[i], fac_s.at[i], fac_r.at[i], other_core).wait_send()


def on_device(Z, K, tokens, gate_codes, up_codes, down_codes, gate_scale, up_scale, down_scale, sign_bits):
    feats = tokens.shape[1]
    width = gate_codes.shape[1]
    NCH = width // BLOCK
    NP = K * YL
    half = Z // 2
    NY = YH * YL
    NX = NP // NY
    dma = pltpu.SemaphoreType.DMA
    any_spec = pl.BlockSpec(memory_space=pl.ANY)
    vmem_spec = pl.BlockSpec(memory_space=pltpu.VMEM)
    return pl.pallas_call(
        functools.partial(kernel, (Z, K, NCH)),
        out_shape=jax.ShapeDtypeStruct(tokens.shape, BF16),
        in_specs=[any_spec] * 7 + [vmem_spec],
        out_specs=vmem_spec,
        scratch_shapes=[
            pltpu.VMEM((2, 2, NX, YH, Z, ROWS, feats // 2), BF16),
            pltpu.VMEM((NCH, 2, 2, feats, BLOCK), BF16),
            pltpu.VMEM((2, NCH, 2, TILE, feats), BF16),
            pltpu.VMEM((3, 2 * NCH, TILE), jnp.int32),
            pltpu.VMEM((NCH, Z, 2, K * ROWS, BLOCK), BF16),
            pltpu.VMEM((2, NCH, half, 2, K * ROWS, BLOCK), BF16),
            pltpu.VMEM((NCH, 2, K, ROWS, TILE), BF16),
            pltpu.VMEM((NCH, NP, ROWS, TILE), BF16),
            pltpu.VMEM((NCH, NP, ROWS, TILE), BF16),
            pltpu.VMEM((Z, NCH, 2, K, ROWS, TILE), BF16),
            pltpu.VMEM((Z, NX, NY, ROWS, feats // 2), BF16),
            pltpu.VMEM((Z, NY, NX, ROWS, feats // 2), BF16),
            pltpu.VMEM((Z, NX, NY, ROWS, feats // 2), BF16),
            pltpu.VMEM((Z, NY, NX, ROWS, feats // 2), BF16),
            pltpu.VMEM((Z, NY, ROWS, feats // 2), BF16),
            pltpu.VMEM((Z, NX, ROWS, feats // 2), BF16),
            pltpu.VMEM((Z, NY, ROWS, feats // 2), BF16),
            pltpu.VMEM((Z, NX, ROWS, feats // 2), BF16),
            pltpu.VMEM((BLOCK, BLOCK), BF16),
            dma((2, 2, 2, 4)), dma((2, 2, 2, 4)), dma((2, Z)),
            dma((NCH,)), dma((NCH,)), dma((NCH,)), dma((NCH,)),
            dma, dma, dma, dma,
            dma((3,)), dma((3,)),
            dma((2, NCH, half)), dma((2, NCH, half)),
            dma((NCH,)), dma((NCH,)), dma((NCH,)), dma((NCH,)),
            dma((2, NCH, half)), dma((2, NCH, half)),
            dma((2, 2)), dma((2, Z)), dma((2,)),
        ],
        compiler_params=pltpu.CompilerParams(
            collective_id=0, has_side_effects=True, vmem_limit_bytes=56 * 1024 * 1024),
    )(
        tokens.reshape(Z, ROWS, feats),
        gate_codes,
        up_codes,
        down_codes.reshape(NCH, 2, TILE, down_codes.shape[1]),
        gate_scale.reshape(2 * NCH, TILE),
        up_scale.reshape(2 * NCH, TILE),
        sign_bits.reshape(2 * NCH, TILE),
        down_scale.reshape(feats // TILE, TILE),
    )


def solution(mesh):
    Z = mesh.shape["seq"] // YL
    K = mesh.shape["tensor"] // CORES
    placed = (
        P("tensor", "seq"),
        P("seq", "tensor"),
        P("seq", "tensor"),
        P("tensor", "seq"),
        P("tensor"),
        P("tensor"),
        P("seq"),
        P("tensor"),
    )
    return jax.shard_map(
        functools.partial(on_device, Z, K), mesh=mesh, in_specs=placed, out_specs=P("tensor", "seq"), check_vma=False
    )
```

```python
import functools
import math

import jax
import jax.numpy as jnp
from jax import lax
from jax.experimental import pallas as pl
from jax.experimental.pallas import tpu as pltpu
from jax.sharding import PartitionSpec as P

BLOCK = 256
TILE = 128
ROWS = 16
YL = 2
YH = 2
CORES = 2
CODE_SCALE = 2.0 ** (-24)
MESH = pl.DeviceIdType.MESH
F32 = jnp.float32
BF16 = jnp.bfloat16


def kernel(
    cfg,
    tok_hbm, gate_hbm, up_hbm, down_hbm, gs_hbm, us_hbm, sb_hbm, ds_ref,
    out_ref,
    tok, wv, dv, fac, part, ring, lr, ar, br, agr, dp0, dp1, o1x, o1y, v0, v1, o2x, o2y, wtab,
    tok_s, tok_r, tok_o, wa, wb, w_s, wf_s, d_a, d_b, d_s, df_s, fac_r, fac_s,
    ring_s, ring_r, a_s, a_r, b_s, b_r, g_s, g_r, o_s, o1_r, o2_r,
):
    Z, K, NCH = cfg
    NP = K * YL
    half = Z // 2
    seq = lax.axis_index("seq")
    ten = lax.axis_index("tensor")
    z = seq // YL
    a = lax.rem(seq, YL)
    k = ten // CORES
    c = lax.rem(ten, CORES)
    me = k * YL + a
    diag = a == c

    def plane(p):
        return (z * YL + lax.rem(p, YL), (p // YL) * CORES + c)

    def ring_dev(d):
        step = 1 if d == 0 else Z - 1
        return (lax.rem(z + step, Z) * YL + a, ten)

    other_core = (seq, k * CORES + (1 - c))
    other_y = (z * YL + (1 - a), ten)

    def remote(src, dst, ss, rs, dev):
        return pltpu.make_async_remote_copy(
            src_ref=src, dst_ref=dst, send_sem=ss, recv_sem=rs,
            device_id=dev, device_id_type=MESH)

    NY = YH * YL
    NX = NP // NY
    x, y = k // YH, lax.rem(k, YH) * YL + a

    def chip(cx, cy):
        return (z * YL + lax.rem(cy, YL), (cx * YH + cy // YL) * CORES + c)

    def moved(axis, by):
        if axis == 0:
            return lax.rem(x + by, NX), y
        return x, lax.rem(y + by, NY)

    barrier = pltpu.get_barrier_semaphore()
    peers = [chip(*moved(0, i)) for i in range(1, NX)] + [chip(*moved(1, i)) for i in range(1, NY)]
    peers += [other_core, ring_dev(0), ring_dev(1)]
    for dev in peers:
        pl.semaphore_signal(barrier, inc=1, device_id=dev, device_id_type=MESH)

    far = sorted(range(Z), key=lambda step: abs(step - half))
    place = {step: r for r, step in enumerate(far)}
    feats = down_hbm.shape[-1]
    wide = feats // 2

    def tok_own(f, r):
        return pltpu.make_async_copy(
            tok_hbm.at[lax.rem(z + far[r], Z), :, f * wide:(f + 1) * wide], tok.at[a, f, x, y // YL, r], tok_o.at[f, r])

    for f in range(2):
        for r in range(Z):
            tok_own(f, r).start()

    bits = lax.broadcasted_iota(jnp.int32, (BLOCK, BLOCK), 0) & lax.broadcasted_iota(jnp.int32, (BLOCK, BLOCK), 1)
    for by in (4, 2, 1):
        bits = bits ^ (bits >> by)
    wtab[...] = (1 - 2 * (bits & 1)).astype(F32).astype(BF16)

    for f in range(2):
        for r in range(Z):
            tok_own(f, r).wait()
    pl.semaphore_wait(barrier, len(peers))

    here = (x, y)
    sizes = (NX, NY)
    some = Z // 2

    def tok_copy(piece, f, stage, i, source=False):
        rows = pl.ds(piece * some, some)
        axis = f if stage == 0 else 1 - f
        by = sizes[axis] - i if source else i
        cx, cy = moved(axis, by)
        dev = chip(cx, cy)
        if not source:
            cx, cy = x, y
        if stage == 0:
            ref = tok.at[lax.rem(cy, YL), f, cx, cy // YL, rows]
        elif f == 0:
            ref = tok.at[lax.rem(cy, YL), f, :, cy // YL, rows]
        else:
            ref = tok.at[:, f, cx, :, rows]
        sem = (piece, f, stage, i)
        return remote(ref, ref, tok_s.at[sem], tok_r.at[sem], dev)

    def tok_each(do, piece, stage):
        for i in (1, 3, 2):
            for f in range(2):
                if i < sizes[f if stage == 0 else 1 - f]:
                    do(piece, f, stage, i)

    def tok_send(piece, stage):
        tok_each(lambda *at: tok_copy(*at).start(), piece, stage)

    def tok_take(piece, stage):
        tok_each(lambda *at: tok_copy(*at, source=True).wait_recv(), piece, stage)

    def tok_sent():
        for piece in range(2):
            for stage in range(2):
                tok_each(lambda *at: tok_copy(*at).wait_send(), piece, stage)

    tok_send(0, 0)
    tok_send(1, 0)

    def chunk_of(ref, ch):
        return ref.at[:, pl.ds(pl.multiple_of(ch * BLOCK, BLOCK), BLOCK)]

    def w_start(ch):
        for g, ref in enumerate((gate_hbm, up_hbm)):
            src = chunk_of(ref, ch)
            dst = wv.at[ch, a, g]

            @pl.when(diag)
            def _():
                pltpu.make_async_copy(src, dst, wa.at[ch]).start()
                remote(src, dst, w_s.at[ch], wa.at[ch], other_core).start()

            @pl.when(jnp.logical_not(diag))
            def _():
                remote(src, dst, w_s.at[ch], wb.at[ch], other_y).start()

    def w_wait(ch):
        pltpu.make_async_copy(wv.at[ch, a], wv.at[ch, a], wa.at[ch]).wait()
        pltpu.make_async_copy(wv.at[ch, 1 - a], wv.at[ch, 1 - a], wb.at[ch]).wait()

    def w_forward(ch):
        return remote(wv.at[ch, 1 - a], wv.at[ch, 1 - a], wf_s.at[ch], wb.at[ch], other_core)

    def d_start():
        @pl.when(diag)
        def _():
            pltpu.make_async_copy(down_hbm, dv.at[a], d_a).start()
            remote(down_hbm, dv.at[a], d_s, d_a, other_core).start()

        @pl.when(jnp.logical_not(diag))
        def _():
            remote(down_hbm, dv.at[a], d_s, d_b, other_y).start()

    def d_wait():
        pltpu.make_async_copy(dv.at[a], dv.at[a], d_a).wait()
        pltpu.make_async_copy(dv.at[1 - a], dv.at[1 - a], d_b).wait()

    def d_forward():
        return remote(dv.at[1 - a], dv.at[1 - a], df_s, d_b, other_core)

    ahead = min(3, NCH)
    w_start(0)

    @pl.when(diag)
    def _():
        for i, ref in enumerate((gs_hbm, us_hbm, sb_hbm)):
            pltpu.make_async_copy(ref, fac.at[i], fac_r.at[i]).start()
            remote(ref, fac.at[i], fac_s.at[i], fac_r.at[i], other_core).start()

    for piece in range(2):
        tok_take(piece, 0)
        tok_send(piece, 1)
    for ch in range(1, ahead):
        w_start(ch)
    tok_take(0, 1)
    for i in range(3):
        pltpu.make_async_copy(fac.at[i], fac.at[i], fac_r.at[i]).wait()

    def ring_copy(d, ch, n):
        j = place[half - n if d == 0 else Z - half + n]
        if n == 0:
            return remote(part.at[ch, j, d], ring.at[d, ch, n, d], ring_s.at[d, ch, n], ring_r.at[d, ch, n], ring_dev(d))
        return remote(part.at[ch, j], ring.at[d, ch, n], ring_s.at[d, ch, n], ring_r.at[d, ch, n], ring_dev(d))

    def product_rows(ch, lo, hi):
        def rows(m, _):
            for g in range(2):
                acc = jnp.zeros((2 * K * ROWS, BLOCK), F32)
                for f in range(2):
                    for q in range(2):
                        xs = [tok[f, q, :, :, 2 * m + e].reshape(K * ROWS, wide) for e in range(2)]
                        acc += jnp.dot(jnp.concatenate(xs, axis=0), wv[ch, f, g, q * wide:(q + 1) * wide],
                                       preferred_element_type=F32)
                part[ch, pl.ds(2 * m, 2), g] = acc.astype(BF16).reshape(2, K * ROWS, BLOCK)
            return 0

        lax.fori_loop(lo // 2, hi // 2, rows, 0)

    def w_take(ch):
        w_wait(ch)

        @pl.when(diag)
        def _():
            w_forward(ch).start()

    def w_next(ch):
        @pl.when(ch + ahead < NCH)
        def _():
            w_start(ch + ahead)

        @pl.when(ch == NCH - 1)
        def _():
            d_start()

    def product(ch):
        w_take(ch)
        product_rows(ch, 0, Z)
        w_next(ch)

    def ring_first(ch):
        for d in range(2):
            ring_copy(d, ch, 0).start()

    def middle(ch, n):
        for d in range(2):
            ring_copy(d, ch, n - 1).wait_recv()
            j = place[half - n if d == 0 else Z - half + n]
            for g in ((d,) if n == 1 else (0, 1)):
                part[ch, j, g] = (part[ch, j, g].astype(F32) + ring[d, ch, n - 1, g].astype(F32)).astype(BF16)
            ring_copy(d, ch, n).start()

    def last(ch):
        n = half - 1
        for d in range(2):
            ring_copy(d, ch, n).wait_recv()
        sums = [
            part[ch, place[0], g].astype(F32) + ring[0, ch, n, g].astype(F32) + ring[1, ch, n, g].astype(F32)
            for g in range(2)
        ]
        gate_f, up_f, sign = [
            jnp.concatenate([fac[i, pl.ds(2 * ch + h, 1), :] for h in range(2)], axis=1) for i in range(3)
        ]
        gate = sums[0] * (gate_f.astype(F32) * CODE_SCALE)
        up = sums[1] * (up_f.astype(F32) * CODE_SCALE)
        hidden = gate / (1.0 + jnp.exp(-gate)) * up * (2 * sign - 1).astype(F32)
        hi = hidden.astype(BF16)
        lo = (hidden - hi.astype(F32)).astype(BF16)
        w = wtab[...]
        turned = jnp.dot(hi, w, preferred_element_type=F32) + jnp.dot(lo, w, preferred_element_type=F32)
        turned = (turned * (1.0 / math.sqrt(BLOCK))).astype(BF16)
        for h in range(2):
            lr[ch, h] = turned[:, h * TILE:(h + 1) * TILE].reshape(K, ROWS, TILE)

    my_r, my_h = me // 2, lax.rem(me, 2)

    def a_copy(ch, i):
        p = lax.rem(me + i, NP)
        return remote(lr.at[ch, lax.rem(p, 2), p // 2], ar.at[ch, me], a_s.at[ch], a_r.at[ch], plane(p))

    def b_copy(ch, i):
        p = lax.rem(me + i, NP)
        return remote(br.at[ch, p], agr.at[z, ch, my_h, my_r], b_s.at[ch], b_r.at[ch], plane(p))

    def others(copy, ch):
        def start(i, _):
            copy(ch, i).start()
            return 0

        lax.fori_loop(1, NP, start, 0)

    def all_others(sem):
        pltpu.make_async_copy(ar.at[0, 1:NP], ar.at[0, 1:NP], sem).wait()

    def a_send(ch):
        others(a_copy, ch)
        ar[ch, me] = lr[ch, my_h, my_r]

    def mix(ch):
        all_others(a_r.at[ch])
        vals = [ar[ch, q].astype(F32) for q in range(NP)]
        bit = 1
        while bit < NP:
            nxt = list(vals)
            for q in range(NP):
                if not q & bit:
                    nxt[q] = vals[q] + vals[q | bit]
                    nxt[q | bit] = vals[q] - vals[q | bit]
            vals = nxt
            bit *= 2
        for q in range(NP):
            br[ch, q] = (vals[q] * (1.0 / math.sqrt(NP))).astype(BF16)
        others(b_copy, ch)
        agr[z, ch, my_h, my_r] = br[ch, me]

    def g_copy(d, ch, n):
        j = lax.rem(z + (Z - n if d == 0 else n), Z)
        ref = agr.at[j, ch] if n < half - 1 else agr.at[j, ch, d]
        return remote(ref, ref, g_s.at[d, ch, n], g_r.at[d, ch, n], ring_dev(d))

    def g_wait(d, ch, n):
        j = lax.rem(z + (2 * Z - 1 - n if d == 0 else 1 + n), Z)
        ref = agr.at[j, ch] if n < half - 1 else agr.at[j, ch, d]
        pltpu.make_async_copy(ref, ref, g_r.at[d, ch, n]).wait()

    def g_send(ch, n):
        for d in range(2):
            g_copy(d, ch, n).start()

    def g_take(ch, n):
        for d in range(2):
            g_wait(d, ch, n)
            if n + 1 < half:
                g_copy(d, ch, n + 1).start()

    quarter = wide

    def o_copy(f, stage, j, i):
        axis = f if stage == 0 else 1 - f
        p = lax.rem(here[axis] + i, sizes[axis])
        dev = chip(p, y) if axis == 0 else chip(x, p)
        if stage == 0:
            return remote((dp0, dp1)[f].at[j, p], (o1x, o1y)[f].at[j, here[axis]], o_s.at[f, 0], o1_r.at[f, j], dev)
        return remote((v0, v1)[f].at[j, p], (o2x, o2y)[f].at[j, here[axis]], o_s.at[f, 1], o2_r.at[f], dev)

    def down(j):
        x_all = jnp.concatenate(
            [agr[j, ch, h].reshape(K * ROWS, TILE) for ch in range(NCH) for h in range(2)], axis=1)
        for f in range(2):
            for e in range(2):
                cols = slice(f * quarter, (f + 1) * quarter)
                acc = jnp.dot(x_all, dv[e, :, :, :, cols].reshape(NCH * BLOCK, quarter), preferred_element_type=F32)
                acc = acc.astype(BF16).reshape(NX, YH, ROWS, quarter)
                for yh in range(YH):
                    if f == 0:
                        dp0[j, :, yh * YL + e] = acc[:, yh]
                    else:
                        dp1[j, yh * YL + e] = acc[:, yh]
            for i in range(1, sizes[f]):
                o_copy(f, 0, j, i).start()
        o1x[j, x] = dp0[j, x]
        o1y[j, y] = dp1[j, y]

    def second(j):
        for f in range(2):
            src = (o1x, o1y)[f]
            got = src.at[j, 1:sizes[f]]
            pltpu.make_async_copy(got, got, o1_r.at[f, j]).wait()
            acc = src[j, 0].astype(F32)
            for q in range(1, sizes[f]):
                acc += src[j, q].astype(F32)
            dst = (v0, v1)[f]
            dst[j] = acc.astype(BF16)
            for i in range(1, sizes[1 - f]):
                o_copy(f, 1, j, i).start()
        o2x[j, y] = v0[j, y]
        o2y[j, x] = v1[j, x]

    def near(do, n):
        def one(i, _):
            do(lax.rem(z + jnp.where(i == 0, Z - 1 - n, 1 + n), Z))
            return 0

        lax.fori_loop(0, 2 if n < half - 1 else 1, one, 0)

    final = NCH - 1 + half + 2

    def slot(t, _):
        def at(n, do):
            ch = t - n

            @pl.when(jnp.logical_and(ch >= 0, ch < NCH))
            def _():
                do(ch)

        def back(ch):
            all_others(b_r.at[ch])
            g_send(ch, 0)

        at(0, ring_first)
        for n in range(half - 1, 0, -1):
            at(n, functools.partial(middle, n=n))
        for n in range(half, -1, -1):
            at(half + 2 + n, functools.partial(g_take, n=n - 1) if n else back)
        at(half + 1, mix)
        at(half, last)
        at(half, a_send)
        at(-1, product)

        @pl.when(t == final - 2)
        def _():
            @pl.when(diag)
            def _():
                d_wait()
                d_forward().start()

        @pl.when(jnp.logical_and(t == final, jnp.logical_not(diag)))
        def _():
            d_wait()

        @pl.when(t == final)
        def _():
            down(z)

        for n in range(half):
            @pl.when(t == final + 1 + n)
            def _():
                near(down, n)
                if n == 0:
                    second(z)
                else:
                    near(second, n - 1)

        return 0

    w_take(0)
    product_rows(0, 0, some)
    ring_first(0)
    tok_take(1, 1)
    product_rows(0, some, Z)
    w_next(0)
    product(1)
    lax.fori_loop(1, final + half + 1, slot, 0)
    near(second, half - 1)

    for f in range(2):
        got = (o2x, o2y)[f].at[:, 1:sizes[1 - f]]
        pltpu.make_async_copy(got, got, o2_r.at[f]).wait()

    def total(j, _):
        for f in range(2):
            src = (o2x, o2y)[f]
            acc = src[j, 0].astype(F32)
            for q in range(1, sizes[1 - f]):
                acc += src[j, q].astype(F32)
            per = quarter // TILE
            scale = jnp.concatenate([ds_ref[f * per + i:f * per + i + 1, :] for i in range(per)], axis=1)
            out_ref[pl.ds(pl.multiple_of(j * ROWS, ROWS), ROWS), f * quarter:(f + 1) * quarter] = (
                acc * (scale.astype(F32) * CODE_SCALE)).astype(BF16)
        return 0

    lax.fori_loop(0, Z, total, 0)

    for f in range(2):
        for i, out in enumerate(((o1x, o1y)[f].at[:, 1:sizes[f]], (o2x, o2y)[f].at[:, 1:sizes[1 - f]])):
            pltpu.make_async_copy(out, out, o_s.at[f, i]).wait()
    tok_sent()

    def w_sent(ch, _):
        pltpu.make_async_copy(wv.at[ch, a], wv.at[ch, a], w_s.at[ch]).wait()

        @pl.when(diag)
        def _():
            w_forward(ch).wait_send()

        for d in range(2):
            for n in range(half):
                ring_copy(d, ch, n).wait_send()
                g_copy(d, ch, n).wait_send()
        all_others(a_s.at[ch])
        all_others(b_s.at[ch])
        return 0

    lax.fori_loop(0, NCH, w_sent, 0)
    pltpu.make_async_copy(dv.at[a], dv.at[a], d_s).wait()

    @pl.when(diag)
    def _():
        d_forward().wait_send()
        for i, ref in enumerate((gs_hbm, us_hbm, sb_hbm)):
            remote(ref, fac.at[i], fac_s.at[i], fac_r.at[i], other_core).wait_send()


def on_device(Z, K, tokens, gate_codes, up_codes, down_codes, gate_scale, up_scale, down_scale, sign_bits):
    feats = tokens.shape[1]
    width = gate_codes.shape[1]
    NCH = width // BLOCK
    NP = K * YL
    half = Z // 2
    NY = YH * YL
    NX = NP // NY
    dma = pltpu.SemaphoreType.DMA
    any_spec = pl.BlockSpec(memory_space=pl.ANY)
    vmem_spec = pl.BlockSpec(memory_space=pltpu.VMEM)
    return pl.pallas_call(
        functools.partial(kernel, (Z, K, NCH)),
        out_shape=jax.ShapeDtypeStruct(tokens.shape, BF16),
        in_specs=[any_spec] * 7 + [vmem_spec],
        out_specs=vmem_spec,
        scratch_shapes=[
            pltpu.VMEM((2, 2, NX, YH, Z, ROWS, feats // 2), BF16),
            pltpu.VMEM((NCH, 2, 2, feats, BLOCK), BF16),
            pltpu.VMEM((2, NCH, 2, TILE, feats), BF16),
            pltpu.VMEM((3, 2 * NCH, TILE), jnp.int32),
            pltpu.VMEM((NCH, Z, 2, K * ROWS, BLOCK), BF16),
            pltpu.VMEM((2, NCH, half, 2, K * ROWS, BLOCK), BF16),
            pltpu.VMEM((NCH, 2, K, ROWS, TILE), BF16),
            pltpu.VMEM((NCH, NP, ROWS, TILE), BF16),
            pltpu.VMEM((NCH, NP, ROWS, TILE), BF16),
            pltpu.VMEM((Z, NCH, 2, K, ROWS, TILE), BF16),
            pltpu.VMEM((Z, NX, NY, ROWS, feats // 2), BF16),
            pltpu.VMEM((Z, NY, NX, ROWS, feats // 2), BF16),
            pltpu.VMEM((Z, NX, NY, ROWS, feats // 2), BF16),
            pltpu.VMEM((Z, NY, NX, ROWS, feats // 2), BF16),
            pltpu.VMEM((Z, NY, ROWS, feats // 2), BF16),
            pltpu.VMEM((Z, NX, ROWS, feats // 2), BF16),
            pltpu.VMEM((Z, NY, ROWS, feats // 2), BF16),
            pltpu.VMEM((Z, NX, ROWS, feats // 2), BF16),
            pltpu.VMEM((BLOCK, BLOCK), BF16),
            dma((2, 2, 2, 4)), dma((2, 2, 2, 4)), dma((2, Z)),
            dma((NCH,)), dma((NCH,)), dma((NCH,)), dma((NCH,)),
            dma, dma, dma, dma,
            dma((3,)), dma((3,)),
            dma((2, NCH, half)), dma((2, NCH, half)),
            dma((NCH,)), dma((NCH,)), dma((NCH,)), dma((NCH,)),
            dma((2, NCH, half)), dma((2, NCH, half)),
            dma((2, 2)), dma((2, Z)), dma((2,)),
        ],
        compiler_params=pltpu.CompilerParams(
            collective_id=0, has_side_effects=True, vmem_limit_bytes=56 * 1024 * 1024),
    )(
        tokens.reshape(Z, ROWS, feats),
        gate_codes,
        up_codes,
        down_codes.reshape(NCH, 2, TILE, down_codes.shape[1]),
        gate_scale.reshape(2 * NCH, TILE),
        up_scale.reshape(2 * NCH, TILE),
        sign_bits.reshape(2 * NCH, TILE),
        down_scale.reshape(feats // TILE, TILE),
    )


def solution(mesh):
    Z = mesh.shape["seq"] // YL
    K = mesh.shape["tensor"] // CORES
    placed = (
        P("tensor", "seq"),
        P("seq", "tensor"),
        P("seq", "tensor"),
        P("tensor", "seq"),
        P("tensor"),
        P("tensor"),
        P("seq"),
        P("tensor"),
    )
    return jax.shard_map(
        functools.partial(on_device, Z, K), mesh=mesh, in_specs=placed, out_specs=P("tensor", "seq"), check_vma=False
    )
```
